512 devices in a mesh: row: 32 (over z, x), col: 16 (over y, core).
Axes of the slice: x: 4, y: 8, z: 8, core: 2. Of those that a mesh axis runs over, the one named last changes fastest.
Arguments:
- inv_diag: float32 [32, 4, 16, 8], P('row', None, 'col'), may hold values from -0.25 to 2, as said below
- panel: float32 [16, 8, 32, 3072], P('col', None, 'row'), may hold values from -2 to 2
- slab: float32 [32, 32, 16, 6144], P('row', None, 'col'), may hold values from -6 to 6
Outputs:
- updated: float32 [32, 32, 16, 6144], P('row', None, 'col')
The draws below stay inside these ranges and needn't reach their ends.
Inputs may be any that keep to these rules, and one draw needn't show every extreme that they name: inv_diag holds a lower-triangular matrix with positive diagonal, entry (i, k) at [i % 32, i // 32, k % 16, k // 16].
All inputs are finite; a program needn't handle non-finite values.
Results may differ from the reference program's by a relative error of at most 0.00008.
Values sent between devices are 32-bit elements; how exact they have to be, the bound alone decides.
A program may use at most 64 MiB of HBM per device.

```python
import jax
import jax.numpy as jnp
from jax import lax

NB = 128
N2 = 98304
SR_DEV = 32
N_ROW = 32
N_COL = 16


def draw_inv_diag(key, part):
    key = jax.random.fold_in(key, 5)
    first, second = jax.random.split(key)
    index = jnp.arange(NB)
    lower = index[:, None] > index[None, :]
    diag_vals = jax.random.uniform(first, (NB,), jnp.float32, 0.6, 1.6)
    off_vals = jnp.clip(jax.random.normal(second, (NB, NB), jnp.float32), -4.0, 4.0) * 0.06
    full = jnp.where(lower, off_vals, 0.0) + jnp.diag(diag_vals)
    return full.reshape(NB // N_ROW, N_ROW, NB // N_COL, N_COL).transpose(1, 0, 3, 2)


def block_levels(key, shape, pieces, smallest, top_value):
    def one(position, parts):
        steps = jax.random.uniform(jax.random.fold_in(jax.random.fold_in(key, 6), position), (parts,), jnp.float32, smallest / len(pieces), top_value / len(pieces))
        return jnp.repeat(jnp.exp(steps), shape[position] // parts).reshape((-1,) + (1,) * (len(shape) - position - 1))

    gain = one(*pieces[0])
    for cut in pieces[1:]:
        gain = gain * one(*cut)
    return gain


def scatter_about(own_key, dims, scale, reach, pieces=(), held_as=jnp.bfloat16):
    drawn = scale * jax.random.normal(own_key, dims, jnp.float32)
    if pieces:
        drawn = drawn * block_levels(own_key, dims, pieces, -0.22, 0.18)
    return jnp.clip(drawn, -reach, reach).astype(held_as)


def setup_inputs(seed: int = 0) -> dict:
    seeds = jax.random.split(jax.random.key(seed), 4)
    return {
        "inv_diag": draw_inv_diag(jax.random.fold_in(seeds[3], 71), 0),
        "panel": scatter_about(seeds[1], (N_COL, NB // N_COL, N_ROW, N2 // N_ROW), 0.3, 2.0, ((0, 16), (2, 32)), jnp.float32),
        "slab": scatter_about(seeds[2], (N_ROW, SR_DEV, N_COL, N2 // N_COL), 1.0, 6.0, ((0, 32), (2, 16)), jnp.float32),
    }


def reference(inv_diag, panel, slab):
    inverse = inv_diag.transpose(1, 0, 3, 2).reshape(NB, NB)
    block_col = panel.transpose(3, 2, 1, 0).reshape(N2, NB)
    factor = jnp.dot(block_col, inverse.T, precision=lax.Precision.HIGHEST, preferred_element_type=jnp.float32)
    rows_all = slab.transpose(1, 0, 3, 2).reshape(SR_DEV * N_ROW, N2)
    upper = factor[0:SR_DEV * N_ROW]
    result = rows_all - jnp.dot(upper, factor.T, precision=lax.Precision.HIGHEST, preferred_element_type=jnp.float32)
    return result.reshape(SR_DEV, N_ROW, N2 // N_COL, N_COL).transpose(1, 0, 3, 2)
```

```python
import functools

import jax
import jax.numpy as jnp
from jax import lax
from jax.experimental import pallas as pl
from jax.experimental.pallas import tpu as pltpu
from jax.sharding import PartitionSpec as P

MESH = pl.DeviceIdType.MESH
NB = 128
NX, NY, NZ = 4, 8, 8
NC = 16
NR = 32
HALF = 1536
Q = 3
CW = HALF // Q
DZ = (1, -1, 3, -3)
F32 = jnp.float32
BF16 = jnp.bfloat16


def kernel(
    inv_ref,
    panel_ref,
    slab_ref,
    out_ref,
    inv_v,
    panel_lin,
    panel_t,
    slab_lin,
    slab_t,
    mine,
    gath,
    rowset,
    m_all,
    a_x,
    data,
    outb,
    urecv,
    out_lin,
    in_sem,
    out_sem,
    ga_send,
    ga_recv,
    gb_send,
    gb_recv,
    ax_send,
    ax_recv,
    sc_send,
    sc_recv,
    fw_send,
    ex_send,
    ex_recv,
):
    row = lax.axis_index("row")
    col = lax.axis_index("col")
    x = lax.rem(row, NX)
    z = lax.div(row, NX)
    y = lax.div(col, 2)
    core = lax.rem(col, 2)

    def dev(dx, dy, dz, dk):
        return (lax.rem(dz, NZ) * NX + lax.rem(dx, NX), lax.rem(dy, NY) * 2 + dk)

    def remote(src, dst, ss, rs, device):
        return pltpu.make_async_remote_copy(
            src_ref=src, dst_ref=dst, send_sem=ss, recv_sem=rs, device_id=device, device_id_type=MESH
        )

    my_member = lax.div(z, 4)
    to_x = jnp.where(my_member == 0, x, 3 - x)
    to_y = 2 * lax.rem(z, 4) + lax.div(x, 2)
    member = jnp.where(lax.div(x, 2) == lax.rem(y, 2), 0, 1)
    from_x = jnp.where(member == 0, x, 3 - x)
    from_z = lax.div(y, 2) + 4 * member
    to_core = lax.rem(from_x, 2)
    first = lax.rem(z + from_z, 2) == 1

    loads = [
        pltpu.make_async_copy(inv_ref, inv_v, in_sem.at[0]),
        pltpu.make_async_copy(panel_ref, panel_lin, in_sem.at[1]),
        pltpu.make_async_copy(slab_ref, slab_lin, in_sem.at[2]),
    ]
    for load in loads:
        load.start()

    barrier = pltpu.get_barrier_semaphore()

    def hello(device):
        pl.semaphore_signal(barrier, inc=1, device_id=device, device_id_type=MESH)

    @pl.when(first)
    def _():
        for i in range(NC):
            hello((from_z * NX + from_x, lax.rem(col + i, NC)))

    for i in range(1, NR):
        hello((lax.rem(row + i, NR), col))
    for i in range(1, NC):
        hello((row, lax.rem(col + i, NC)))
    for i in range(1, NX):
        hello(dev(x + i, y, z, 1 - core))

    lane = lax.broadcasted_iota(jnp.int32, (8, 128), 1)
    mine[...] = jnp.zeros_like(mine)
    loads[0].wait()
    for i in range(4):
        mine[i : i + 1, 0:8] = inv_v[0, i, :, :]
    placed = pltpu.roll(mine[0:8, :], col * 8, 1)
    mine[0:8, :] = placed
    loads[1].wait()
    head = panel_lin[pl.ds(0, 8, stride=24), :]
    mine[8:16, :] = pltpu.roll(jnp.where(lane < 32, head, 0.0), x * 32, 1)
    gath[pl.ds(col, 1)] = mine[...].reshape(1, 16, 128)
    perm = lax.div(lane, 2) + 64 * lax.rem(lane + my_member, 2)
    for b in range(24):
        tile = panel_lin[pl.ds(b, 8, stride=24), :]
        panel_t[:, b * 128 : (b + 1) * 128] = jnp.take_along_axis(tile, perm, axis=1)

    pl.semaphore_wait(barrier, 2 * len(DZ) + (NR - 1) + (NC - 1) + (NX - 1))

    for i in range(1, NC):
        remote(mine, gath.at[col], ga_send.at[0], ga_recv.at[0], (row, lax.rem(col + i, NC))).start()

    my_k = pl.multiple_of(col * 8, 8)
    scatter = []
    for q in range(Q):
        for d, dz in enumerate(DZ):
            for h in range(2):
                cp = remote(
                    panel_t.at[:, pl.ds(h * HALF + q * CW, CW)],
                    data.at[pl.ds(my_k, 8), pl.ds(q * CW, CW)],
                    sc_send.at[q, d, h],
                    sc_recv.at[col, q],
                    dev(to_x, to_y, z + dz + NZ, h),
                )
                cp.start()
                scatter.append(cp)

    loads[2].wait()
    for g in range(4):
        for b in range(48):
            slab_t[g * 8 : (g + 1) * 8, b * 128 : (b + 1) * 128] = slab_lin[pl.ds(g * 8 * 48 + b, 8, stride=48), :]

    pltpu.make_async_copy(gath.at[pl.ds(0, NC - 1)], gath.at[pl.ds(0, NC - 1)], ga_recv.at[0]).wait()
    rows = gath[0, 0:8, :]
    for i in range(1, NC):
        rows = rows + gath[i, 0:8, :]
    rowset[...] = rows
    my_r = pl.multiple_of(row * 8, 8)
    for i in range(1, NR):
        remote(rowset, m_all.at[pl.ds(my_r, 8)], gb_send.at[0], gb_recv.at[0], (lax.rem(row + i, NR), col)).start()
    m_all[pl.ds(my_r, 8), :] = rows
    for i in range(NC):
        a_x[x, i * 8 : (i + 1) * 8, :] = gath[i, 8:16, :]
    for i in range(1, NX):
        remote(a_x.at[x], a_x.at[x], ax_send.at[0], ax_recv.at[0], dev(x + i, y, z, core)).start()

    def arrived(c, q):
        piece = data.at[pl.ds(pl.multiple_of(c * 8, 8), 8), pl.ds(q * CW, CW)]
        pltpu.make_async_copy(piece, piece, sc_recv.at[c, q]).wait()
        return piece

    order = (0, 1, 7, 2, 6, 3, 5, 4)

    def forwards(q):
        out = []
        for dy in order:
            for k in range(2):
                c = lax.rem(y + dy, NY) * 2 + k
                piece = data.at[pl.ds(pl.multiple_of(c * 8, 8), 8), pl.ds(q * CW, CW)]
                out.append(
                    (c, remote(piece, piece, fw_send.at[c, q], sc_recv.at[c, q], dev(x, y, z + (1 if k == 0 else NZ - 1), core)))
                )
        return out

    for q in range(Q):

        @pl.when(first)
        def _():
            for c, cp in forwards(q):
                arrived(c, q)
                cp.start()

    pltpu.make_async_copy(a_x.at[pl.ds(0, 3)], a_x.at[pl.ds(0, 3)], ax_recv.at[0]).wait()
    heads = (a_x[0] + a_x[1] + a_x[2] + a_x[3]).T
    pltpu.make_async_copy(m_all.at[pl.ds(0, 8 * (NR - 1))], m_all.at[pl.ds(0, 8 * (NR - 1))], gb_recv.at[0]).wait()
    inverse = m_all[...]
    gram = jnp.dot(inverse.T, inverse, precision=lax.Precision.HIGHEST, preferred_element_type=F32)
    w = jnp.dot(heads, gram, precision=lax.Precision.HIGHEST, preferred_element_type=F32)
    wh = w.astype(BF16)
    wl = (w - wh.astype(F32)).astype(BF16)
    wcat = jnp.concatenate([wh, wl], axis=0)

    exchange = []
    for q in range(Q):

        @pl.when(jnp.logical_not(first))
        def _():
            for dy in order:
                for k in range(2):
                    arrived(lax.rem(y + dy, NY) * 2 + k, q)

        a = data[:, q * CW : (q + 1) * CW]
        ah = a.astype(BF16)
        al = (a - ah.astype(F32)).astype(BF16)
        both = jnp.dot(wcat, ah, preferred_element_type=F32)
        outb[q] = both[0:NB] + both[NB:] + jnp.dot(wh, al, preferred_element_type=F32)
        for i in range(1, NX):
            other = lax.rem(x + i, NX)
            cp = remote(
                outb.at[q, pl.ds(pl.multiple_of(other * 32, 32), 32)],
                urecv.at[member, core, q],
                ex_send.at[i, q],
                ex_recv.at[member, core, q],
                dev(x + i, y, z, to_core),
            )
            cp.start()
            exchange.append(cp)
        own = outb.at[q, pl.ds(pl.multiple_of(x * 32, 32), 32)]

        @pl.when(to_core == core)
        def _():
            pltpu.make_async_copy(own, urecv.at[member, core, q], ex_recv.at[member, core, q]).start()

        @pl.when(to_core != core)
        def _():
            remote(
                own, urecv.at[member, core, q], ex_send.at[0, q], ex_recv.at[member, core, q], dev(x, y, z, 1 - core)
            ).start()

    even = lax.rem(lane, 2) == 0
    swap = lane + 1 - 2 * lax.rem(lane, 2)
    for q in range(Q):
        for h in range(2):
            for m in range(2):
                slot = urecv.at[m, h, q]
                pltpu.make_async_copy(slot, slot, ex_recv.at[m, h, q]).wait()
            for t in range(CW // 128):
                b = 24 * h + 2 * (q * (CW // 128) + t)
                for g in range(4):
                    u0 = urecv[0, h, q, g * 8 : (g + 1) * 8, t * 128 : (t + 1) * 128]
                    u1 = urecv[1, h, q, g * 8 : (g + 1) * 8, t * 128 : (t + 1) * 128]
                    low = jnp.where(even, u0, u1)
                    high = jnp.take_along_axis(jnp.where(even, u1, u0), swap, axis=1)
                    s0 = slab_t[g * 8 : (g + 1) * 8, b * 128 : (b + 1) * 128]
                    s1 = slab_t[g * 8 : (g + 1) * 8, (b + 1) * 128 : (b + 2) * 128]
                    out_lin[pl.ds(g * 8 * 48 + b, 8, stride=48), :] = s0 - low
                    out_lin[pl.ds(g * 8 * 48 + b + 1, 8, stride=48), :] = s1 - high
    store = pltpu.make_async_copy(out_lin, out_ref, out_sem)
    store.start()

    for q in range(Q):

        @pl.when(first)
        def _():
            for _, cp in forwards(q):
                cp.wait_send()

        @pl.when(to_core != core)
        def _():
            own = outb.at[q, pl.ds(0, 32)]
            pltpu.make_async_copy(own, own, ex_send.at[0, q]).wait()

    for cp in scatter + exchange:
        cp.wait_send()
    pltpu.make_async_copy(gath.at[pl.ds(0, NC - 1)], gath.at[pl.ds(0, NC - 1)], ga_send.at[0]).wait()
    pltpu.make_async_copy(m_all.at[pl.ds(0, 8 * (NR - 1))], m_all.at[pl.ds(0, 8 * (NR - 1))], gb_send.at[0]).wait()
    pltpu.make_async_copy(a_x.at[pl.ds(0, 3)], a_x.at[pl.ds(0, 3)], ax_send.at[0]).wait()
    store.wait()


def body(inv_diag, panel, slab):
    dma = pltpu.SemaphoreType.DMA
    out = pl.pallas_call(
        kernel,
        out_shape=jax.ShapeDtypeStruct((1536, 128), F32),
        in_specs=[pl.BlockSpec(memory_space=pl.ANY)] * 3,
        out_specs=pl.BlockSpec(memory_space=pl.ANY),
        scratch_shapes=[
            pltpu.VMEM((1, 4, 1, 8), F32),
            pltpu.VMEM((192, 128), F32),
            pltpu.VMEM((8, 3072), F32),
            pltpu.VMEM((1536, 128), F32),
            pltpu.VMEM((32, 6144), F32),
            pltpu.VMEM((16, 128), F32),
            pltpu.VMEM((NC, 16, 128), F32),
            pltpu.VMEM((8, 128), F32),
            pltpu.VMEM((NR * 8, 128), F32),
            pltpu.VMEM((NX, NB, 128), F32),
            pltpu.VMEM((NB, HALF), F32),
            pltpu.VMEM((Q, NB, CW), F32),
            pltpu.VMEM((2, 2, Q, 32, CW), F32),
            pltpu.VMEM((1536, 128), F32),
            dma((3,)),
            dma,
            dma((1,)),
            dma((1,)),
            dma((1,)),
            dma((1,)),
            dma((1,)),
            dma((1,)),
            dma((Q, len(DZ), 2)),
            dma((NC, Q)),
            dma((NC, Q)),
            dma((NX, Q)),
            dma((2, 2, Q)),
        ],
        compiler_params=pltpu.CompilerParams(
            collective_id=0, has_side_effects=True, vmem_limit_bytes=40 * 2**20
        ),
        cost_estimate=pl.CostEstimate(flops=200_000_000, bytes_accessed=1_700_000, transcendentals=0),
        name="panel_step",
    )(inv_diag, panel.reshape(192, 128), slab.reshape(1536, 128))
    return out.reshape(slab.shape)


def solution(mesh):
    return jax.shard_map(
        body,
        mesh=mesh,
        in_specs=(
            P("row", None, "col", None),
            P("col", None, "row", None),
            P("row", None, "col", None),
        ),
        out_specs=P("row", None, "col", None),
        check_vma=False,
    )
```

```python
import jax
import jax.numpy as jnp
from jax import lax
from jax.experimental import pallas as pl
from jax.experimental.pallas import tpu as pltpu
from jax.sharding import PartitionSpec as P

MESH = pl.DeviceIdType.MESH
NB = 128
NX, NY, NZ = 4, 8, 8
NC = 16
NR = 32
HALF = 1536
NQ = 4
CW = HALF // NQ
F32 = jnp.float32
BF16 = jnp.bfloat16
COLS = sorted(range(1, NC), key=lambda i: -min(i // 2, NY - i // 2))
ROWS = sorted(
    [(i, j) for i in range(NX) for j in range(NZ) if i or j],
    key=lambda s: -(min(s[0], NX - s[0]) + min(s[1], NZ - s[1])),
)
PLACE = [(c // 2 % 2) * 8 + c // 4 * 2 + c % 2 for c in range(NC)]


def kernel(
    inv_ref,
    panel_ref,
    slab_ref,
    out_ref,
    inv_v,
    panel_lin,
    panel_t,
    slab_lin,
    slab_t,
    mine,
    gath,
    rowset,
    m_all,
    a_x,
    data,
    outb,
    urecv,
    in_sem,
    ga_send,
    ga_recv,
    gb_send,
    gb_recv,
    ax_send,
    ax_recv,
    sc_send,
    blk_recv,
    ag_send,
    ex_send,
    ex_recv,
):
    row = lax.axis_index("row")
    col = lax.axis_index("col")
    x = lax.rem(row, NX)
    z = lax.div(row, NX)
    y = lax.div(col, 2)
    core = lax.rem(col, 2)

    def dev(dx, dy, dz, dk):
        return (lax.rem(dz, NZ) * NX + lax.rem(dx, NX), lax.rem(dy, NY) * 2 + dk)

    def remote(src, dst, ss, rs, device):
        return pltpu.make_async_remote_copy(
            src_ref=src, dst_ref=dst, send_sem=ss, recv_sem=rs, device_id=device, device_id_type=MESH
        )

    def settle(ref, sem):
        pltpu.make_async_copy(ref, ref, sem).wait()

    my_member = lax.div(z, 4)
    to_x = jnp.where(my_member == 0, x, 3 - x)
    to_y = 2 * lax.rem(z, 4) + lax.div(x, 2)
    member = jnp.where(lax.div(x, 2) == lax.rem(y, 2), 0, 1)
    from_x = jnp.where(member == 0, x, 3 - x)
    from_z = lax.div(y, 2) + 4 * member
    to_core = lax.rem(from_x, 2)
    side = lax.rem(y, 2)
    at_home = (to_x == x) & (to_y == y)
    stays = jnp.where(at_home & (side == lax.rem(z, 2)), 1, 0)

    loads = [
        pltpu.make_async_copy(inv_ref, inv_v, in_sem.at[0]),
        pltpu.make_async_copy(panel_ref, panel_lin, in_sem.at[1]),
        pltpu.make_async_copy(slab_ref, slab_lin, in_sem.at[2]),
    ]
    for load in loads:
        load.start()

    barrier = pltpu.get_barrier_semaphore()

    def hello(device):
        pl.semaphore_signal(barrier, inc=1, device_id=device, device_id_type=MESH)

    for u in range(4):
        for k in range(2):
            source = (from_z * NX + from_x, (2 * u + lax.rem(z, 2)) * 2 + k)

            @pl.when((source[0] != row) | (source[1] != col))
            def _():
                hello(source)

    for i, j in ROWS:
        hello(dev(x + i, y, z + j, core))
    for i in COLS:
        hello((row, lax.rem(col + i, NC)))
    for i in (2, 1, 3):
        hello(dev(x + i, y, z, 1 - core))

    lane = lax.broadcasted_iota(jnp.int32, (8, 128), 1)
    my_place = side * 8 + lax.div(y, 2) * 2 + core
    mine[...] = jnp.zeros_like(mine)
    loads[0].wait()
    for i in range(4):
        mine[i : i + 1, 0:8] = inv_v[0, i, :, :]
    placed = pltpu.roll(mine[0:8, :], my_place * 8, 1)
    mine[0:8, :] = placed
    loads[1].wait()
    head = panel_lin[pl.ds(0, 8, stride=24), :]
    mine[8:16, :] = pltpu.roll(jnp.where(lane < 32, head, 0.0), x * 32, 1)
    gath[pl.ds(col, 1)] = mine[...].reshape(1, 16, 128)
    perm = lax.div(lane, 2) + 64 * lax.rem(lane + my_member, 2)
    for b in range(24):
        tile = panel_lin[pl.ds(b, 8, stride=24), :]
        panel_t[:, b * 128 : (b + 1) * 128] = jnp.take_along_axis(tile, perm, axis=1)

    pl.semaphore_wait(barrier, 8 - stays + (NR - 1) + (NC - 1) + (NX - 1))

    for i in COLS:
        remote(mine, gath.at[col], ga_send.at[0], ga_recv.at[0], (row, lax.rem(col + i, NC))).start()

    my_u = lax.div(y, 2)
    my_rows = pl.ds(pl.multiple_of((my_u * 2 + core) * 8, 8), 8)

    def piece(q, h):
        return panel_t.at[:, pl.ds(h * HALF + q * CW, CW)]

    for q in range(NQ):
        s = 2 * q + side
        for h in range(2):
            here = (stays == 1) & (s == z) & (core == h)

            @pl.when(here)
            def _():
                pltpu.make_async_copy(piece(q, h), data.at[s, my_rows], blk_recv.at[s, my_u]).start()

            @pl.when(jnp.logical_not(here))
            def _():
                remote(
                    piece(q, h), data.at[s, my_rows], sc_send.at[q, h], blk_recv.at[s, my_u], dev(to_x, to_y, s, h)
                ).start()

    loads[2].wait()
    for g in range(4):
        for b in range(48):
            slab_t[g * 8 : (g + 1) * 8, b * 128 : (b + 1) * 128] = slab_lin[pl.ds(g * 8 * 48 + b, 8, stride=48), :]

    settle(gath.at[pl.ds(0, NC - 1)], ga_recv.at[0])
    rows = gath[0, 0:8, :]
    for i in range(1, NC):
        rows = rows + gath[i, 0:8, :]
    rowset[...] = rows
    my_r = pl.multiple_of(row * 8, 8)
    for i, j in ROWS:
        remote(rowset, m_all.at[pl.ds(my_r, 8)], gb_send.at[0], gb_recv.at[0], dev(x + i, y, z + j, core)).start()
    m_all[pl.ds(my_r, 8), :] = rows
    for i in range(NC):
        a_x[x, PLACE[i] * 8 : (PLACE[i] + 1) * 8, :] = gath[i, 8:16, :]
    for i in (2, 1, 3):
        remote(a_x.at[x], a_x.at[x], ax_send.at[0], ax_recv.at[0], dev(x + i, y, z, core)).start()

    odd = lax.rem(y + z, 2)
    subs = []
    for near, far in ((0, 1), (2, -1), (-2, 3), (4, -3)):
        yy = lax.rem(y + jnp.where(odd == 0, near, far) + NY, NY)
        subs.append(lax.div(yy, 2))

    def block(s, u):
        return data.at[s, pl.ds(pl.multiple_of(u * 16, 16), 16)]

    def pass_on(s, u, n, dz):
        return remote(block(s, u), block(s, u), ag_send.at[n], blk_recv.at[s, u], dev(x, y, z + dz + NZ, core))

    def have(s, u):
        settle(block(s, u), blk_recv.at[s, u])

    below = lax.rem(z + NZ - 2, NZ)
    above = lax.rem(z + 2, NZ)
    plan = []
    for i, u in enumerate(subs):
        plan.append((z, u, [2, -2, 1, -1]))
    for i, u in enumerate(subs):
        plan.append((below, u, [2, 1] if i in (0, 3) else [1]))
        plan.append((above, u, [-2, -1] if i in (1, 2) else [-1]))
    passed = []
    for s, u, steps in plan:
        have(s, u)
        for dz in steps:
            cp = pass_on(s, u, len(passed), dz)
            cp.start()
            passed.append(cp)

    settle(a_x.at[pl.ds(0, 3)], ax_recv.at[0])
    heads = (a_x[0] + a_x[1] + a_x[2] + a_x[3]).T
    settle(m_all.at[pl.ds(0, 8 * (NR - 1))], gb_recv.at[0])
    inverse = m_all[...]
    gram = jnp.dot(inverse.T, inverse, precision=lax.Precision.HIGHEST, preferred_element_type=F32)
    w = jnp.dot(heads, gram, precision=lax.Precision.HIGHEST, preferred_element_type=F32)
    wh = w.astype(BF16)
    wl = (w - wh.astype(F32)).astype(BF16)
    wcat = jnp.concatenate([wh, wl], axis=0)

    mine_q = lax.div(z, 2)
    lean = jnp.where(lax.rem(z, 2) == 0, 3, 1)
    chunks = [mine_q, lax.rem(mine_q + lean, NQ), lax.rem(mine_q + 4 - lean, NQ), lax.rem(mine_q + 2, NQ)]

    def late(s):
        return (s != z) & (s != below) & (s != above)

    exchange = []
    for n, q in enumerate(chunks):
        for half in range(2):
            s = 2 * q + half

            @pl.when(late(s))
            def _():
                for u in range(4):
                    have(s, u)

        a = jnp.concatenate([data[2 * q], data[2 * q + 1]], axis=0)
        ah = a.astype(BF16)
        al = (a - ah.astype(F32)).astype(BF16)
        both = jnp.dot(wcat, ah, preferred_element_type=F32)
        outb[n] = both[0:NB] + both[NB:] + jnp.dot(wh, al, preferred_element_type=F32)
        for i in (2, 1, 3):
            other = lax.rem(x + i, NX)
            cp = remote(
                outb.at[n, pl.ds(pl.multiple_of(other * 32, 32), 32)],
                urecv.at[member, core, n],
                ex_send.at[i, n],
                ex_recv.at[member, core, n],
                dev(x + i, y, z, to_core),
            )
            cp.start()
            exchange.append(cp)
        own = outb.at[n, pl.ds(pl.multiple_of(x * 32, 32), 32)]

        @pl.when(to_core == core)
        def _():
            pltpu.make_async_copy(own, urecv.at[member, core, n], ex_recv.at[member, core, n]).start()

        @pl.when(to_core != core)
        def _():
            remote(
                own, urecv.at[member, core, n], ex_send.at[0, n], ex_recv.at[member, core, n], dev(x, y, z, 1 - core)
            ).start()

    even = lax.rem(lane, 2) == 0
    swap = lane + 1 - 2 * lax.rem(lane, 2)
    for n, q in enumerate(chunks):
        for h in range(2):
            for m in range(2):
                settle(urecv.at[m, h, n], ex_recv.at[m, h, n])
            for t in range(CW // 128):
                b = 24 * h + 2 * (q * (CW // 128) + t)
                for g in range(4):
                    u0 = urecv[0, h, n, g * 8 : (g + 1) * 8, t * 128 : (t + 1) * 128]
                    u1 = urecv[1, h, n, g * 8 : (g + 1) * 8, t * 128 : (t + 1) * 128]
                    low = jnp.where(even, u0, u1)
                    high = jnp.take_along_axis(jnp.where(even, u1, u0), swap, axis=1)
                    s0 = slab_t[g * 8 : (g + 1) * 8, pl.ds(pl.multiple_of(b * 128, 128), 128)]
                    s1 = slab_t[g * 8 : (g + 1) * 8, pl.ds(pl.multiple_of(b * 128 + 128, 128), 128)]
                    out_ref[pl.ds(g * 8 * 48 + b, 8, stride=48), :] = s0 - low
                    out_ref[pl.ds(g * 8 * 48 + b + 1, 8, stride=48), :] = s1 - high

    for q in range(NQ):
        for h in range(2):
            here = (stays == 1) & (2 * q + side == z) & (core == h)

            @pl.when(jnp.logical_not(here))
            def _():
                settle(piece(q, h), sc_send.at[q, h])

    @pl.when(to_core != core)
    def _():
        for n in range(NQ):
            settle(outb.at[n, pl.ds(0, 32)], ex_send.at[0, n])

    for cp in passed + exchange:
        cp.wait_send()
    settle(gath.at[pl.ds(0, NC - 1)], ga_send.at[0])
    settle(m_all.at[pl.ds(0, 8 * (NR - 1))], gb_send.at[0])
    settle(a_x.at[pl.ds(0, 3)], ax_send.at[0])


def body(inv_diag, panel, slab):
    dma = pltpu.SemaphoreType.DMA
    out = pl.pallas_call(
        kernel,
        out_shape=jax.ShapeDtypeStruct((1536, 128), F32),
        in_specs=[pl.BlockSpec(memory_space=pl.ANY)] * 3,
        out_specs=pl.BlockSpec(memory_space=pltpu.VMEM),
        scratch_shapes=[
            pltpu.VMEM((1, 4, 1, 8), F32),
            pltpu.VMEM((192, 128), F32),
            pltpu.VMEM((8, 3072), F32),
            pltpu.VMEM((1536, 128), F32),
            pltpu.VMEM((32, 6144), F32),
            pltpu.VMEM((16, 128), F32),
            pltpu.VMEM((NC, 16, 128), F32),
            pltpu.VMEM((8, 128), F32),
            pltpu.VMEM((NR * 8, 128), F32),
            pltpu.VMEM((NX, NB, 128), F32),
            pltpu.VMEM((8, 64, CW), F32),
            pltpu.VMEM((NQ, NB, CW), F32),
            pltpu.VMEM((2, 2, NQ, 32, CW), F32),
            dma((3,)),
            dma((1,)),
            dma((1,)),
            dma((1,)),
            dma((1,)),
            dma((1,)),
            dma((1,)),
            dma((NQ, 2)),
            dma((8, 4)),
            dma((28,)),
            dma((NX, NQ)),
            dma((2, 2, NQ)),
        ],
        compiler_params=pltpu.CompilerParams(
            collective_id=0, has_side_effects=True, vmem_limit_bytes=60 * 2**20
        ),
        cost_estimate=pl.CostEstimate(flops=200_000_000, bytes_accessed=1_700_000, transcendentals=0),
        name="panel_step",
    )(inv_diag, panel.reshape(192, 128), slab.reshape(1536, 128))
    return out.reshape(slab.shape)


def solution(mesh):
    return jax.shard_map(
        body,
        mesh=mesh,
        in_specs=(
            P("row", None, "col", None),
            P("col", None, "row", None),
            P("row", None, "col", None),
        ),
        out_specs=P("row", None, "col", None),
        check_vma=False,
    )
```

```python
import jax
import jax.numpy as jnp
from jax import lax
from jax.experimental import pallas as pl
from jax.experimental.pallas import tpu as pltpu
from jax.sharding import PartitionSpec as P

MESH = pl.DeviceIdType.MESH
NB = 128
NX, NY, NZ = 4, 8, 8
NC = 16
NR = 32
HALF = 1536
NQ = 4
CW = HALF // NQ
W_AT = 8
FIRST_AT = 10
F32 = jnp.float32
BF16 = jnp.bfloat16
COLS = sorted(range(1, NC), key=lambda i: -min(i // 2, NY - i // 2))
ROWS = sorted(
    [(i, j) for i in range(NX) for j in range(NZ) if i or j],
    key=lambda s: -(min(s[0], NX - s[0]) + min(s[1], NZ - s[1])),
)
PLACE = [(c // 2 % 2) * 8 + c // 4 * 2 + c % 2 for c in range(NC)]


def kernel(
    inv_ref,
    panel_ref,
    slab_ref,
    out_ref,
    inv_v,
    panel_lin,
    panel_t,
    slab_lin,
    slab_t,
    mine,
    gath,
    rowset,
    m_all,
    a_x,
    stage,
    data,
    outb,
    urecv,
    wcat,
    in_sem,
    ga_send,
    ga_recv,
    gb_send,
    gb_recv,
    ax_send,
    ax_recv,
    za_send,
    za_recv,
    sc_send,
    blk_recv,
    ag_send,
    ex_send,
    ex_recv,
):
    row = lax.axis_index("row")
    col = lax.axis_index("col")
    x = lax.rem(row, NX)
    z = lax.div(row, NX)
    y = lax.div(col, 2)
    core = lax.rem(col, 2)

    def dev(dx, dy, dz, dk):
        return (lax.rem(dz, NZ) * NX + lax.rem(dx, NX), lax.rem(dy, NY) * 2 + dk)

    def remote(src, dst, ss, rs, device):
        return pltpu.make_async_remote_copy(
            src_ref=src, dst_ref=dst, send_sem=ss, recv_sem=rs, device_id=device, device_id_type=MESH
        )

    def settle(ref, sem):
        pltpu.make_async_copy(ref, ref, sem).wait()

    my_member = lax.div(z, 4)
    member = jnp.where(lax.div(x, 2) == lax.rem(y, 2), 0, 1)
    from_x = jnp.where(member == 0, x, 3 - x)
    from_z = lax.div(y, 2) + 4 * member
    to_core = lax.rem(from_x, 2)
    side = lax.rem(y, 2)
    active = side == lax.rem(z, 2)

    loads = [
        pltpu.make_async_copy(inv_ref, inv_v, in_sem.at[0]),
        pltpu.make_async_copy(panel_ref, panel_lin, in_sem.at[1]),
        pltpu.make_async_copy(slab_ref, slab_lin, in_sem.at[2]),
    ]
    for load in loads:
        load.start()

    barrier = pltpu.get_barrier_semaphore()

    def hello(device):
        pl.semaphore_signal(barrier, inc=1, device_id=device, device_id_type=MESH)

    own_too = jnp.where((from_x == x) & active, 1, 0)
    for u in range(4):
        for k in range(2):
            source = (z * NX + from_x, (2 * u + lax.rem(z, 2)) * 2 + k)

            @pl.when((source[0] != row) | (source[1] != col))
            def _():
                hello(source)

    for i, j in ROWS:
        hello(dev(x + i, y, z + j, core))
    for i in COLS:
        hello((row, lax.rem(col + i, NC)))
    for i in (2, 1, 3):
        hello(dev(x + i, y, z, 1 - core))

    lane = lax.broadcasted_iota(jnp.int32, (8, 128), 1)
    my_place = side * 8 + lax.div(y, 2) * 2 + core
    mine[...] = jnp.zeros_like(mine)
    loads[0].wait()
    for i in range(4):
        mine[i : i + 1, 0:8] = inv_v[0, i, :, :]
    placed = pltpu.roll(mine[0:8, :], my_place * 8, 1)
    mine[0:8, :] = placed
    loads[1].wait()
    head = panel_lin[pl.ds(0, 8, stride=24), :]
    mine[8:16, :] = pltpu.roll(jnp.where(lane < 32, head, 0.0), x * 32, 1)
    gath[pl.ds(col, 1)] = mine[...].reshape(1, 16, 128)
    perm = lax.div(lane, 2) + 64 * lax.rem(lane + my_member, 2)
    for q in range(NQ):
        for h in range(2):
            for t in range(3):
                tile = panel_lin[pl.ds(12 * h + 3 * q + t, 8, stride=24), :]
                panel_t[q, :, (3 * h + t) * 128 : (3 * h + t + 1) * 128] = jnp.take_along_axis(tile, perm, axis=1)

    pl.semaphore_wait(barrier, jnp.where(active, 16, 0) - own_too + (NR - 1) + (NC - 1) + (NX - 1))

    for q in range(NQ):
        zq = 2 * q + side

        @pl.when(zq == z)
        def _():
            pltpu.make_async_copy(panel_t.at[q], stage.at[z], za_recv.at[z]).start()

        @pl.when(zq != z)
        def _():
            remote(panel_t.at[q], stage.at[z], za_send.at[q], za_recv.at[z], dev(x, y, zq, core)).start()

    for i in COLS:
        remote(mine, gath.at[col], ga_send.at[0], ga_recv.at[0], (row, lax.rem(col + i, NC))).start()

    loads[2].wait()
    for g in range(4):
        for b in range(48):
            slab_t[g * 8 : (g + 1) * 8, b * 128 : (b + 1) * 128] = slab_lin[pl.ds(g * 8 * 48 + b, 8, stride=48), :]

    my_u = lax.div(y, 2)
    my_rows = pl.ds(pl.multiple_of((my_u * 2 + core) * 8, 8), 8)

    def hop(n, h):
        src = lax.rem(z + n, NZ)
        goes_x = jnp.where(src < 4, x, 3 - x)
        goes_y = 2 * lax.rem(src, 4) + lax.div(x, 2)
        piece = stage.at[src, :, pl.ds(h * CW, CW)]
        here = (goes_x == x) & (goes_y == y) & (core == h)
        return src, goes_x, goes_y, piece, here

    @pl.when(active)
    def _():
        for n in (0, 1, 7, 2, 6, 3, 5, 4):
            src = hop(n, 0)[0]
            settle(stage.at[src], za_recv.at[src])
            for h in range(2):
                _, goes_x, goes_y, piece, here = hop(n, h)

                @pl.when(here)
                def _():
                    pltpu.make_async_copy(piece, data.at[z, my_rows], blk_recv.at[z, my_u]).start()

                @pl.when(jnp.logical_not(here))
                def _():
                    remote(
                        piece, data.at[z, my_rows], sc_send.at[n, h], blk_recv.at[z, my_u], dev(goes_x, goes_y, z, h)
                    ).start()

    settle(gath.at[pl.ds(0, NC - 1)], ga_recv.at[0])
    rows = gath[0, 0:8, :]
    for i in range(1, NC):
        rows = rows + gath[i, 0:8, :]
    rowset[...] = rows
    my_r = pl.multiple_of(row * 8, 8)
    for i, j in ROWS:
        remote(rowset, m_all.at[pl.ds(my_r, 8)], gb_send.at[0], gb_recv.at[0], dev(x + i, y, z + j, core)).start()
    m_all[pl.ds(my_r, 8), :] = rows
    for i in range(NC):
        a_x[x, PLACE[i] * 8 : (PLACE[i] + 1) * 8, :] = gath[i, 8:16, :]
    for i in (2, 1, 3):
        remote(a_x.at[x], a_x.at[x], ax_send.at[0], ax_recv.at[0], dev(x + i, y, z, core)).start()

    odd = lax.rem(y + z, 2)
    subs = []
    for near, far in ((0, 1), (2, -1), (-2, 3), (4, -3)):
        yy = lax.rem(y + jnp.where(odd == 0, near, far) + NY, NY)
        subs.append(lax.div(yy, 2))

    def block(s, u):
        return data.at[s, pl.ds(pl.multiple_of(u * 16, 16), 16)]

    def pass_on(s, u, n, dz):
        return remote(block(s, u), block(s, u), ag_send.at[n], blk_recv.at[s, u], dev(x, y, z + dz + NZ, core))

    def have(s, u):
        settle(block(s, u), blk_recv.at[s, u])

    below = lax.rem(z + NZ - 2, NZ)
    above = lax.rem(z + 2, NZ)
    plan = []
    for i, u in enumerate(subs):
        plan.append((z, u, [2, -2, 1, -1]))
    for i, u in enumerate(subs):
        plan.append((below, u, [2, 1] if i in (0, 3) else [1]))
        plan.append((above, u, [-2, -1] if i in (1, 2) else [-1]))

    def weights():
        settle(a_x.at[pl.ds(0, 3)], ax_recv.at[0])
        heads = (a_x[0] + a_x[1] + a_x[2] + a_x[3]).T
        settle(m_all.at[pl.ds(0, 8 * (NR - 1))], gb_recv.at[0])
        inverse = m_all[...]
        gram = jnp.dot(inverse.T, inverse, precision=lax.Precision.HIGHEST, preferred_element_type=F32)
        w = jnp.dot(heads, gram, precision=lax.Precision.HIGHEST, preferred_element_type=F32)
        wh = w.astype(BF16)
        wcat[0:NB] = wh
        wcat[NB:] = (w - wh.astype(F32)).astype(BF16)

    mine_q = lax.div(z, 2)
    lean = jnp.where(lax.rem(z, 2) == 0, 3, 1)
    chunks = [mine_q, lax.rem(mine_q + lean, NQ), lax.rem(mine_q + 4 - lean, NQ), lax.rem(mine_q + 2, NQ)]
    exchange = []

    def chunk(n):
        q = chunks[n]
        for half in range(2):
            s = 2 * q + half

            @pl.when((s != z) & (s != below) & (s != above))
            def _():
                for u in range(4):
                    have(s, u)

        a = jnp.concatenate([data[2 * q], data[2 * q + 1]], axis=0)
        ah = a.astype(BF16)
        al = (a - ah.astype(F32)).astype(BF16)
        both = jnp.dot(wcat[...], ah, preferred_element_type=F32)
        outb[n] = both[0:NB] + both[NB:] + jnp.dot(wcat[0:NB], al, preferred_element_type=F32)
        for i in (2, 1, 3):
            other = lax.rem(x + i, NX)
            cp = remote(
                outb.at[n, pl.ds(pl.multiple_of(other * 32, 32), 32)],
                urecv.at[member, core, n],
                ex_send.at[i, n],
                ex_recv.at[member, core, n],
                dev(x + i, y, z, to_core),
            )
            cp.start()
            exchange.append(cp)
        own = outb.at[n, pl.ds(pl.multiple_of(x * 32, 32), 32)]

        @pl.when(to_core == core)
        def _():
            pltpu.make_async_copy(own, urecv.at[member, core, n], ex_recv.at[member, core, n]).start()

        @pl.when(to_core != core)
        def _():
            remote(
                own, urecv.at[member, core, n], ex_send.at[0, n], ex_recv.at[member, core, n], dev(x, y, z, 1 - core)
            ).start()

    passed = []
    for step, (s, u, steps) in enumerate(plan):
        if step == W_AT:
            weights()
        if step == FIRST_AT:
            chunk(0)
        have(s, u)
        for dz in steps:
            cp = pass_on(s, u, len(passed), dz)
            cp.start()
            passed.append(cp)
    if W_AT >= len(plan):
        weights()
    for n in range(1 if FIRST_AT < len(plan) else 0, NQ):
        chunk(n)

    even = lax.rem(lane, 2) == 0
    swap = lane + 1 - 2 * lax.rem(lane, 2)
    for n, q in enumerate(chunks):
        for h in range(2):
            for m in range(2):
                settle(urecv.at[m, h, n], ex_recv.at[m, h, n])
            for t in range(CW // 128):
                b = 24 * h + 2 * (q * (CW // 128) + t)
                for g in range(4):
                    u0 = urecv[0, h, n, g * 8 : (g + 1) * 8, t * 128 : (t + 1) * 128]
                    u1 = urecv[1, h, n, g * 8 : (g + 1) * 8, t * 128 : (t + 1) * 128]
                    low = jnp.where(even, u0, u1)
                    high = jnp.take_along_axis(jnp.where(even, u1, u0), swap, axis=1)
                    s0 = slab_t[g * 8 : (g + 1) * 8, pl.ds(pl.multiple_of(b * 128, 128), 128)]
                    s1 = slab_t[g * 8 : (g + 1) * 8, pl.ds(pl.multiple_of(b * 128 + 128, 128), 128)]
                    out_ref[pl.ds(g * 8 * 48 + b, 8, stride=48), :] = s0 - low
                    out_ref[pl.ds(g * 8 * 48 + b + 1, 8, stride=48), :] = s1 - high

    for q in range(NQ):

        @pl.when(2 * q + side != z)
        def _():
            settle(panel_t.at[q], za_send.at[q])

    @pl.when(active)
    def _():
        for n in range(8):
            for h in range(2):
                _, _, _, piece, here = hop(n, h)

                @pl.when(jnp.logical_not(here))
                def _():
                    settle(piece, sc_send.at[n, h])

    @pl.when(to_core != core)
    def _():
        for n in range(NQ):
            settle(outb.at[n, pl.ds(0, 32)], ex_send.at[0, n])

    for cp in passed + exchange:
        cp.wait_send()
    settle(gath.at[pl.ds(0, NC - 1)], ga_send.at[0])
    settle(m_all.at[pl.ds(0, 8 * (NR - 1))], gb_send.at[0])
    settle(a_x.at[pl.ds(0, 3)], ax_send.at[0])


def body(inv_diag, panel, slab):
    dma = pltpu.SemaphoreType.DMA
    out = pl.pallas_call(
        kernel,
        out_shape=jax.ShapeDtypeStruct((1536, 128), F32),
        in_specs=[pl.BlockSpec(memory_space=pl.ANY)] * 3,
        out_specs=pl.BlockSpec(memory_space=pltpu.VMEM),
        scratch_shapes=[
            pltpu.VMEM((1, 4, 1, 8), F32),
            pltpu.VMEM((192, 128), F32),
            pltpu.VMEM((NQ, 8, 2 * CW), F32),
            pltpu.VMEM((1536, 128), F32),
            pltpu.VMEM((32, 6144), F32),
            pltpu.VMEM((16, 128), F32),
            pltpu.VMEM((NC, 16, 128), F32),
            pltpu.VMEM((8, 128), F32),
            pltpu.VMEM((NR * 8, 128), F32),
            pltpu.VMEM((NX, NB, 128), F32),
            pltpu.VMEM((NZ, 8, 2 * CW), F32),
            pltpu.VMEM((8, 64, CW), F32),
            pltpu.VMEM((NQ, NB, CW), F32),
            pltpu.VMEM((2, 2, NQ, 32, CW), F32),
            pltpu.VMEM((2 * NB, NB), BF16),
            dma((3,)),
            dma((1,)),
            dma((1,)),
            dma((1,)),
            dma((1,)),
            dma((1,)),
            dma((1,)),
            dma((NQ,)),
            dma((NZ,)),
            dma((NZ, 2)),
            dma((8, 4)),
            dma((28,)),
            dma((NX, NQ)),
            dma((2, 2, NQ)),
        ],
        compiler_params=pltpu.CompilerParams(
            collective_id=0, has_side_effects=True, vmem_limit_bytes=60 * 2**20
        ),
        cost_estimate=pl.CostEstimate(flops=200_000_000, bytes_accessed=1_700_000, transcendentals=0),
        name="panel_step",
    )(inv_diag, panel.reshape(192, 128), slab.reshape(1536, 128))
    return out.reshape(slab.shape)


def solution(mesh):
    return jax.shard_map(
        body,
        mesh=mesh,
        in_specs=(
            P("row", None, "col", None),
            P("col", None, "row", None),
            P("row", None, "col", None),
        ),
        out_specs=P("row", None, "col", None),
        check_vma=False,
    )
```

```python
import jax
import jax.numpy as jnp
from jax import lax
from jax.experimental import pallas as pl
from jax.experimental.pallas import tpu as pltpu
from jax.sharding import PartitionSpec as P

MESH = pl.DeviceIdType.MESH
NB = 128
NX, NY, NZ = 4, 8, 8
NC = 16
HALF = 1536
NQ = 4
CW = HALF // NQ
F32 = jnp.float32
BF16 = jnp.bfloat16
COLS = sorted(range(1, NC), key=lambda i: -min(i // 2, NY - i // 2))
ZS = (4, 3, 5, 2, 6, 1, 7)
PLACE = [c % 2 * 8 + c // 2 for c in range(NC)]
ORDER = (
    "h0", "h1", "h7", "h2", "h6", "h3", "h5", "a", "h4", "A0", "H", "A1",
    "b", "A2", "A3", "B0", "W", "B1", "C0", "B2", "B3", "C1", "C2", "C3",
)


def kernel(
    inv_ref,
    panel_ref,
    slab_ref,
    out_ref,
    inv_v,
    panel_lin,
    panel_t,
    slab_lin,
    slab_t,
    mine,
    mine_head,
    gath,
    gath_head,
    m_z,
    m_x,
    a_x,
    stage,
    data,
    outb,
    urecv,
    wcat,
    in_sem,
    ga_send,
    ga_recv,
    gh_send,
    gh_recv,
    gb_send,
    gb_recv,
    gc_send,
    gc_recv,
    ax_send,
    ax_recv,
    za_send,
    za_recv,
    sc_send,
    blk_recv,
    ag_send,
    ex_send,
    ex_recv,
):
    row = lax.axis_index("row")
    col = lax.axis_index("col")
    x = lax.rem(row, NX)
    z = lax.div(row, NX)
    y = lax.div(col, 2)
    core = lax.rem(col, 2)

    def dev(dx, dy, dz, dk):
        return (lax.rem(dz, NZ) * NX + lax.rem(dx, NX), lax.rem(dy, NY) * 2 + dk)

    def remote(src, dst, ss, rs, device):
        return pltpu.make_async_remote_copy(
            src_ref=src, dst_ref=dst, send_sem=ss, recv_sem=rs, device_id=device, device_id_type=MESH
        )

    def settle(ref, sem):
        pltpu.make_async_copy(ref, ref, sem).wait()

    my_member = lax.div(z, 4)
    member = jnp.where(lax.div(x, 2) == lax.rem(y, 2), 0, 1)
    from_x = jnp.where(member == 0, x, 3 - x)
    from_z = lax.div(y, 2) + 4 * member
    to_core = lax.rem(from_x, 2)
    active = core == lax.rem(z, 2)

    loads = [
        pltpu.make_async_copy(inv_ref, inv_v, in_sem.at[0]),
        pltpu.make_async_copy(panel_ref, panel_lin, in_sem.at[1]),
        pltpu.make_async_copy(slab_ref, slab_lin, in_sem.at[2]),
    ]
    for load in loads:
        load.start()

    barrier = pltpu.get_barrier_semaphore()

    def hello(device):
        pl.semaphore_signal(barrier, inc=1, device_id=device, device_id_type=MESH)

    for i in ZS:
        hello(dev(x, y, z + i, core))

    @pl.when(member == 1)
    def _():
        for i in (4, 3, 5, 2, 6, 1, 7, 0):
            hello(dev(from_x, y + i, z, lax.rem(z, 2)))

    for i in COLS:
        hello((row, lax.rem(col + i, NC)))
    for i in (2, 1, 3):
        for k in range(2):
            hello(dev(x + i, y, z, k))

    lane = lax.broadcasted_iota(jnp.int32, (8, 128), 1)
    mine[...] = jnp.zeros_like(mine)
    loads[0].wait()
    for i in range(4):
        mine[i : i + 1, 0:8] = inv_v[0, i, :, :]
    placed = pltpu.roll(pltpu.roll(mine[...], (core * 8 + y) * 8, 1), 4 * lax.rem(z, 2), 0)
    mine[...] = placed
    loads[1].wait()
    head = panel_lin[pl.ds(0, 8, stride=24), :]
    mine_head[...] = pltpu.roll(jnp.where(lane < 32, head, 0.0), x * 32, 1)
    gath_head[pl.ds(col, 1)] = mine_head[...].reshape(1, 8, 128)
    gath[pl.ds(col, 1)] = mine[...].reshape(1, 8, 128)
    perm = lax.div(lane, 2) + 64 * lax.rem(lane + my_member, 2)
    for q in range(NQ):
        for h in range(2):
            for t in range(3):
                tile = panel_lin[pl.ds(12 * h + 3 * q + t, 8, stride=24), :]
                panel_t[q, :, (3 * h + t) * 128 : (3 * h + t + 1) * 128] = jnp.take_along_axis(tile, perm, axis=1)

    pl.semaphore_wait(barrier, (NC - 1) + (NZ - 1) + 2 * (NX - 1) + jnp.where(active, 8, 0))

    for near, far in ((0, 1), (2, -1), (-2, 3), (4, -3)):
        zq = lax.rem(z + jnp.where(active, near, far) + NZ, NZ)
        piece_z = panel_t.at[lax.div(zq, 2)]

        @pl.when(zq == z)
        def _():
            pltpu.make_async_copy(piece_z, stage.at[z], za_recv.at[z]).start()

        @pl.when(zq != z)
        def _():
            remote(piece_z, stage.at[z], za_send.at[0], za_recv.at[z], dev(x, y, zq, core)).start()

    for i in COLS:
        remote(mine, gath.at[col], ga_send.at[0], ga_recv.at[0], (row, lax.rem(col + i, NC))).start()
    for i in COLS:
        remote(
            mine_head, gath_head.at[col], gh_send.at[0], gh_recv.at[0], (row, lax.rem(col + i, NC))
        ).start()

    loads[2].wait()
    for g in range(4):
        for b in range(48):
            slab_t[g * 8 : (g + 1) * 8, b * 128 : (b + 1) * 128] = slab_lin[pl.ds(g * 8 * 48 + b, 8, stride=48), :]

    my_rows = pl.ds(pl.multiple_of(y * 8, 8), 8)

    def hop(n):
        src = lax.rem(z + n, NZ)
        goes_x = jnp.where(src < 4, x, 3 - x)
        goes_y = 2 * lax.rem(src, 4) + lax.div(x, 2)
        at_home = (goes_x == x) & (goes_y == y)
        arrive = blk_recv.at[z, lax.div(y, 2)]

        @pl.when(active)
        def _():
            settle(stage.at[src], za_recv.at[src])
            for h in range(2):
                piece = stage.at[src, :, pl.ds(h * CW, CW)]

                @pl.when(at_home & (core == h))
                def _():
                    pltpu.make_async_copy(piece, data.at[z, my_rows], arrive).start()

                @pl.when(jnp.logical_not(at_home & (core == h)))
                def _():
                    remote(piece, data.at[z, my_rows], sc_send.at[0], arrive, dev(goes_x, goes_y, z, h)).start()

    def inv_along_z():
        settle(gath.at[pl.ds(0, NC - 1)], ga_recv.at[0])
        rows = gath[0]
        for i in range(1, NC):
            rows = rows + gath[i]
        m_z[pl.ds(z, 1)] = rows.reshape(1, 8, 128)
        for i in ZS:
            remote(m_z.at[z], m_z.at[z], gb_send.at[0], gb_recv.at[0], dev(x, y, z + i, core)).start()

    def heads_along_x():
        settle(gath_head.at[pl.ds(0, NC - 1)], gh_recv.at[0])
        for i in range(NC):
            a_x[x, PLACE[i] * 8 : (PLACE[i] + 1) * 8, :] = gath_head[i]
        for i in (2, 1, 3):
            remote(a_x.at[x], a_x.at[x], ax_send.at[0], ax_recv.at[0], dev(x + i, y, z, core)).start()

    def inv_along_x():
        settle(m_z.at[pl.ds(0, NZ - 1)], gb_recv.at[0])
        for j in range(4):
            m_x[x, j * 8 : (j + 1) * 8, :] = m_z[2 * j] + m_z[2 * j + 1]
        for i in (2, 1, 3):
            remote(m_x.at[x], m_x.at[x], gc_send.at[0], gc_recv.at[0], dev(x + i, y, z, core)).start()

    def block(s, u):
        return data.at[s, pl.ds(pl.multiple_of(u * 16, 16), 16)]

    def have(s, u):
        settle(block(s, u), blk_recv.at[s, u])

    def share(s, u, dz):
        remote(block(s, u), block(s, u), ag_send.at[0], blk_recv.at[s, u], dev(x, y, z + dz + NZ, core)).start()

    mine_u = lax.div(y, 2)
    lean_y = jnp.where(lax.rem(y, 2) == 0, 3, 1)
    subs = [mine_u, lax.rem(mine_u + lean_y, 4), lax.rem(mine_u + 4 - lean_y, 4), lax.rem(mine_u + 2, 4)]
    below = lax.rem(z + NZ - 2, NZ)
    above = lax.rem(z + 2, NZ)

    def give(i):
        have(z, subs[i])
        for dz in (1, -1, 2, -2):
            share(z, subs[i], dz)

    def pass_on(i):
        have(below, subs[i])
        for dz in (2, 1) if i in (0, 3) else (1,):
            share(below, subs[i], dz)
        have(above, subs[i])
        for dz in (-2, -1) if i in (1, 2) else (-1,):
            share(above, subs[i], dz)

    def weights():
        settle(a_x.at[pl.ds(0, 3)], ax_recv.at[0])
        heads = (a_x[0] + a_x[1] + a_x[2] + a_x[3]).T
        settle(m_x.at[pl.ds(0, 3)], gc_recv.at[0])
        inverse = m_x[...].reshape(NB, NB)
        gram = jnp.dot(inverse.T, inverse, precision=lax.Precision.HIGHEST, preferred_element_type=F32)
        w = jnp.dot(heads, gram, precision=lax.Precision.HIGHEST, preferred_element_type=F32)
        wh = w.astype(BF16)
        wcat[0:NB] = wh
        wcat[NB:] = (w - wh.astype(F32)).astype(BF16)

    mine_q = lax.div(z, 2)
    lean = jnp.where(lax.rem(z, 2) == 0, 3, 1)
    chunks = [mine_q, lax.rem(mine_q + lean, NQ), lax.rem(mine_q + 4 - lean, NQ), lax.rem(mine_q + 2, NQ)]
    exchange = []

    def chunk(n):
        q = chunks[n]
        for half in range(2):
            s = 2 * q + half

            @pl.when((s != z) & (s != below) & (s != above))
            def _():
                for u in range(4):
                    have(s, u)

        a = jnp.concatenate([data[2 * q], data[2 * q + 1]], axis=0)
        ah = a.astype(BF16)
        al = (a - ah.astype(F32)).astype(BF16)
        both = jnp.dot(wcat[...], ah, preferred_element_type=F32)
        outb[n] = both[0:NB] + both[NB:] + jnp.dot(wcat[0:NB], al, preferred_element_type=F32)
        for i in (2, 1, 3):
            other = lax.rem(x + i, NX)
            cp = remote(
                outb.at[n, pl.ds(pl.multiple_of(other * 32, 32), 32)],
                urecv.at[member, core, n],
                ex_send.at[i, n],
                ex_recv.at[member, core, n],
                dev(x + i, y, z, to_core),
            )
            cp.start()
            exchange.append(cp)
        own = outb.at[n, pl.ds(pl.multiple_of(x * 32, 32), 32)]

        @pl.when(to_core == core)
        def _():
            pltpu.make_async_copy(own, urecv.at[member, core, n], ex_recv.at[member, core, n]).start()

        @pl.when(to_core != core)
        def _():
            remote(
                own, urecv.at[member, core, n], ex_send.at[0, n], ex_recv.at[member, core, n], dev(x, y, z, 1 - core)
            ).start()

    steps = {"h": hop, "a": inv_along_z, "H": heads_along_x, "b": inv_along_x, "A": give, "B": pass_on, "W": weights, "C": chunk}
    for step in ORDER:
        steps[step[0]](*map(int, step[1:]))

    settle(stage.at[pl.ds(0, 3)], za_send.at[0])

    @pl.when(jnp.logical_not(active))
    def _():
        settle(stage.at[0], za_send.at[0])

    @pl.when(active)
    def _():
        settle(stage.at[pl.ds(0, NZ - 1)], sc_send.at[0])
        settle(panel_t.at[0, :, pl.ds(0, CW)], sc_send.at[0])

    @pl.when(active & (member == 1))
    def _():
        settle(panel_t.at[0, :, pl.ds(0, CW)], sc_send.at[0])

    settle(data.at[pl.ds(0, 7)], ag_send.at[0])

    settle(gath.at[pl.ds(0, NC - 1)], ga_send.at[0])
    settle(gath_head.at[pl.ds(0, NC - 1)], gh_send.at[0])
    settle(m_z.at[pl.ds(0, NZ - 1)], gb_send.at[0])
    settle(m_x.at[pl.ds(0, 3)], gc_send.at[0])
    settle(a_x.at[pl.ds(0, 3)], ax_send.at[0])

    even = lax.rem(lane, 2) == 0
    swap = lane + 1 - 2 * lax.rem(lane, 2)
    for n, q in enumerate(chunks):
        for h in range(2):
            for m in range(2):
                settle(urecv.at[m, h, n], ex_recv.at[m, h, n])
            for t in range(CW // 128):
                b = 24 * h + 2 * (q * (CW // 128) + t)
                for g in range(4):
                    u0 = urecv[0, h, n, g * 8 : (g + 1) * 8, t * 128 : (t + 1) * 128]
                    u1 = urecv[1, h, n, g * 8 : (g + 1) * 8, t * 128 : (t + 1) * 128]
                    low = jnp.where(even, u0, u1)
                    high = jnp.take_along_axis(jnp.where(even, u1, u0), swap, axis=1)
                    s0 = slab_t[g * 8 : (g + 1) * 8, pl.ds(pl.multiple_of(b * 128, 128), 128)]
                    s1 = slab_t[g * 8 : (g + 1) * 8, pl.ds(pl.multiple_of(b * 128 + 128, 128), 128)]
                    out_ref[pl.ds(g * 8 * 48 + b, 8, stride=48), :] = s0 - low
                    out_ref[pl.ds(g * 8 * 48 + b + 1, 8, stride=48), :] = s1 - high

        for cp in exchange[3 * n : 3 * n + 3]:
            cp.wait_send()

        @pl.when(to_core != core)
        def _():
            settle(outb.at[n, pl.ds(0, 32)], ex_send.at[0, n])


def body(inv_diag, panel, slab):
    dma = pltpu.SemaphoreType.DMA
    out = pl.pallas_call(
        kernel,
        out_shape=jax.ShapeDtypeStruct((1536, 128), F32),
        in_specs=[pl.BlockSpec(memory_space=pl.ANY)] * 3,
        out_specs=pl.BlockSpec(memory_space=pltpu.VMEM),
        scratch_shapes=[
            pltpu.VMEM((1, 4, 1, 8), F32),
            pltpu.VMEM((192, 128), F32),
            pltpu.VMEM((NQ, 8, 2 * CW), F32),
            pltpu.VMEM((1536, 128), F32),
            pltpu.VMEM((32, 6144), F32),
            pltpu.VMEM((8, 128), F32),
            pltpu.VMEM((8, 128), F32),
            pltpu.VMEM((NC, 8, 128), F32),
            pltpu.VMEM((NC, 8, 128), F32),
            pltpu.VMEM((NZ, 8, 128), F32),
            pltpu.VMEM((NX, 32, 128), F32),
            pltpu.VMEM((NX, NB, 128), F32),
            pltpu.VMEM((NZ, 8, 2 * CW), F32),
            pltpu.VMEM((NZ, NB // 2, CW), F32),
            pltpu.VMEM((NQ, NB, CW), F32),
            pltpu.VMEM((2, 2, NQ, 32, CW), F32),
            pltpu.VMEM((2 * NB, NB), BF16),
            dma((3,)),
            dma((1,)),
            dma((1,)),
            dma((1,)),
            dma((1,)),
            dma((1,)),
            dma((1,)),
            dma((1,)),
            dma((1,)),
            dma((1,)),
            dma((1,)),
            dma((1,)),
            dma((NZ,)),
            dma((1,)),
            dma((NZ, 4)),
            dma((1,)),
            dma((NX, NQ)),
            dma((2, 2, NQ)),
        ],
        compiler_params=pltpu.CompilerParams(
            collective_id=0, has_side_effects=True, vmem_limit_bytes=55_260_000
        ),
        cost_estimate=pl.CostEstimate(flops=200_000_000, bytes_accessed=1_700_000, transcendentals=0),
        name="panel_step",
    )(inv_diag, panel.reshape(192, 128), slab.reshape(1536, 128))
    return out.reshape(slab.shape)


def solution(mesh):
    return jax.shard_map(
        body,
        mesh=mesh,
        in_specs=(
            P("row", None, "col", None),
            P("col", None, "row", None),
            P("row", None, "col", None),
        ),
        out_specs=P("row", None, "col", None),
        check_vma=False,
    )
```

```python
import jax
import jax.numpy as jnp
from jax import lax
from jax.experimental import pallas as pl
from jax.experimental.pallas import tpu as pltpu
from jax.sharding import PartitionSpec as P

MESH = pl.DeviceIdType.MESH
NB = 128
NX, NY, NZ = 4, 8, 8
NC = 16
HALF = 1536
NQ = 4
CW = HALF // NQ
F32 = jnp.float32
BF16 = jnp.bfloat16
COLS = sorted(range(1, NC), key=lambda i: -min(i // 2, NY - i // 2))
ZS = (4, 3, 5, 2, 6, 1, 7)
PLACE = [c % 2 * 8 + c // 2 for c in range(NC)]
ORDER = (
    "h0", "h1", "h7", "h2", "h6", "h3", "h5", "a", "h4", "H",
    "A0", "b", "A1", "B0", "W", "C0", "B1", "C1", "C2", "C3",
)


def kernel(
    inv_ref,
    panel_ref,
    slab_ref,
    out_ref,
    inv_v,
    panel_lin,
    panel_t,
    slab_lin,
    slab_t,
    mine,
    mine_head,
    gath,
    gath_head,
    m_z,
    m_x,
    a_x,
    stage,
    data,
    outb,
    urecv,
    wcat,
    in_sem,
    ga_send,
    ga_recv,
    gh_send,
    gh_recv,
    gb_send,
    gb_recv,
    gc_send,
    gc_recv,
    ax_send,
    ax_recv,
    za_send,
    za_recv,
    sc_send,
    blk_recv,
    ag_send,
    ex_send,
    ex_recv,
):
    row = lax.axis_index("row")
    col = lax.axis_index("col")
    x = lax.rem(row, NX)
    z = lax.div(row, NX)
    y = lax.div(col, 2)
    core = lax.rem(col, 2)

    def dev(dx, dy, dz, dk):
        return (lax.rem(dz, NZ) * NX + lax.rem(dx, NX), lax.rem(dy, NY) * 2 + dk)

    def remote(src, dst, ss, rs, device):
        return pltpu.make_async_remote_copy(
            src_ref=src, dst_ref=dst, send_sem=ss, recv_sem=rs, device_id=device, device_id_type=MESH
        )

    def settle(ref, sem):
        pltpu.make_async_copy(ref, ref, sem).wait()

    my_member = lax.div(z, 4)
    member = jnp.where(lax.div(x, 2) == lax.rem(y, 2), 0, 1)
    from_x = jnp.where(member == 0, x, 3 - x)
    from_z = lax.div(y, 2) + 4 * member
    to_core = lax.rem(from_x, 2)
    active = core == lax.rem(z, 2)

    loads = [
        pltpu.make_async_copy(inv_ref, inv_v, in_sem.at[0]),
        pltpu.make_async_copy(panel_ref, panel_lin, in_sem.at[1]),
        pltpu.make_async_copy(slab_ref, slab_lin, in_sem.at[2]),
    ]
    for load in loads:
        load.start()

    barrier = pltpu.get_barrier_semaphore()

    def hello(device):
        pl.semaphore_signal(barrier, inc=1, device_id=device, device_id_type=MESH)

    for i in ZS:
        hello(dev(x, y, z + i, core))

    @pl.when(member == 1)
    def _():
        for i in (4, 3, 5, 2, 6, 1, 7, 0):
            hello(dev(from_x, y + i, z, lax.rem(z, 2)))

    for i in COLS:
        hello((row, lax.rem(col + i, NC)))
    for i in (2, 1, 3):
        hello(dev(x + i, y, z, core))

    lane = lax.broadcasted_iota(jnp.int32, (8, 128), 1)
    mine[...] = jnp.zeros_like(mine)
    loads[0].wait()
    for i in range(4):
        mine[i : i + 1, 0:8] = inv_v[0, i, :, :]
    placed = pltpu.roll(pltpu.roll(mine[...], (core * 8 + y) * 8, 1), 4 * lax.rem(z, 2), 0)
    mine[...] = placed
    loads[1].wait()
    head = panel_lin[pl.ds(0, 8, stride=24), :]
    mine_head[...] = pltpu.roll(jnp.where(lane < 32, head, 0.0), x * 32, 1)
    gath_head[pl.ds(col, 1)] = mine_head[...].reshape(1, 8, 128)
    gath[pl.ds(col, 1)] = mine[...].reshape(1, 8, 128)
    perm = lax.div(lane, 2) + 64 * lax.rem(lane + my_member, 2)
    for q in range(NQ):
        for h in range(2):
            for t in range(3):
                tile = panel_lin[pl.ds(12 * h + 3 * q + t, 8, stride=24), :]
                panel_t[q, :, (3 * h + t) * 128 : (3 * h + t + 1) * 128] = jnp.take_along_axis(tile, perm, axis=1)

    pl.semaphore_wait(barrier, (NC - 1) + (NZ - 1) + (NX - 1) + jnp.where(active, 8, 0))

    for near, far in ((0, 1), (2, -1), (-2, 3), (4, -3)):
        zq = lax.rem(z + jnp.where(active, near, far) + NZ, NZ)
        piece_z = panel_t.at[lax.div(zq, 2)]

        @pl.when(zq == z)
        def _():
            pltpu.make_async_copy(piece_z, stage.at[z], za_recv.at[z]).start()

        @pl.when(zq != z)
        def _():
            remote(piece_z, stage.at[z], za_send.at[0], za_recv.at[z], dev(x, y, zq, core)).start()

    for i in COLS:
        remote(mine, gath.at[col], ga_send.at[0], ga_recv.at[0], (row, lax.rem(col + i, NC))).start()
    for i in COLS:
        remote(
            mine_head, gath_head.at[col], gh_send.at[0], gh_recv.at[0], (row, lax.rem(col + i, NC))
        ).start()

    loads[2].wait()
    for g in range(4):
        for b in range(48):
            slab_t[g * 8 : (g + 1) * 8, b * 128 : (b + 1) * 128] = slab_lin[pl.ds(g * 8 * 48 + b, 8, stride=48), :]

    my_rows = pl.ds(pl.multiple_of(y * 8, 8), 8)

    def hop(n):
        src = lax.rem(z + n, NZ)
        goes_x = jnp.where(src < 4, x, 3 - x)
        goes_y = 2 * lax.rem(src, 4) + lax.div(x, 2)
        at_home = (goes_x == x) & (goes_y == y)
        arrive = blk_recv.at[z, lax.div(y, 4)]

        @pl.when(active)
        def _():
            settle(stage.at[src], za_recv.at[src])
            for h in range(2):
                piece = stage.at[src, :, pl.ds(h * CW, CW)]

                @pl.when(at_home & (core == h))
                def _():
                    pltpu.make_async_copy(piece, data.at[z, my_rows], arrive).start()

                @pl.when(jnp.logical_not(at_home & (core == h)))
                def _():
                    remote(piece, data.at[z, my_rows], sc_send.at[0], arrive, dev(goes_x, goes_y, z, h)).start()

    def inv_along_z():
        settle(gath.at[pl.ds(0, NC - 1)], ga_recv.at[0])
        rows = gath[0]
        for i in range(1, NC):
            rows = rows + gath[i]
        m_z[pl.ds(z, 1)] = rows.reshape(1, 8, 128)
        for i in ZS:
            remote(m_z.at[z], m_z.at[z], gb_send.at[0], gb_recv.at[0], dev(x, y, z + i, core)).start()

    def heads_along_x():
        settle(gath_head.at[pl.ds(0, NC - 1)], gh_recv.at[0])
        for i in range(NC):
            a_x[x, PLACE[i] * 8 : (PLACE[i] + 1) * 8, :] = gath_head[i]
        for i in (2, 1, 3):
            remote(a_x.at[x], a_x.at[x], ax_send.at[0], ax_recv.at[0], dev(x + i, y, z, core)).start()

    def inv_along_x():
        settle(m_z.at[pl.ds(0, NZ - 1)], gb_recv.at[0])
        for j in range(4):
            m_x[x, j * 8 : (j + 1) * 8, :] = m_z[2 * j] + m_z[2 * j + 1]
        for i in (2, 1, 3):
            remote(m_x.at[x], m_x.at[x], gc_send.at[0], gc_recv.at[0], dev(x + i, y, z, core)).start()

    def block(s, u):
        return data.at[s, pl.ds(pl.multiple_of(u * 32, 32), 32)]

    def have(s, u):
        settle(block(s, u), blk_recv.at[s, u])

    def share(s, u, dz):
        remote(block(s, u), block(s, u), ag_send.at[0], blk_recv.at[s, u], dev(x, y, z + dz + NZ, core)).start()

    subs = [lax.div(y, 4), 1 - lax.div(y, 4)]
    below = lax.rem(z + NZ - 2, NZ)
    above = lax.rem(z + 2, NZ)

    def give(i):
        have(z, subs[i])
        for dz in (1, -1, 2, -2):
            share(z, subs[i], dz)

    def pass_on(i):
        have(below, subs[i])
        for dz in (2, 1) if i == 0 else (1,):
            share(below, subs[i], dz)
        have(above, subs[i])
        for dz in (-2, -1) if i == 1 else (-1,):
            share(above, subs[i], dz)

    def weights():
        settle(a_x.at[pl.ds(0, 3)], ax_recv.at[0])
        heads = (a_x[0] + a_x[1] + a_x[2] + a_x[3]).T
        settle(m_x.at[pl.ds(0, 3)], gc_recv.at[0])
        inverse = m_x[...].reshape(NB, NB)
        gram = jnp.dot(inverse.T, inverse, precision=lax.Precision.HIGHEST, preferred_element_type=F32)
        w = jnp.dot(heads, gram, precision=lax.Precision.HIGHEST, preferred_element_type=F32)
        wh = w.astype(BF16)
        wcat[0:NB] = wh
        wcat[NB:] = (w - wh.astype(F32)).astype(BF16)

    mine_q = lax.div(z, 2)
    lean = jnp.where(lax.rem(z, 2) == 0, 3, 1)
    chunks = [mine_q, lax.rem(mine_q + lean, NQ), lax.rem(mine_q + 4 - lean, NQ), lax.rem(mine_q + 2, NQ)]
    exchange = []

    def chunk(n):
        q = chunks[n]
        for half in range(2):
            s = 2 * q + half

            @pl.when((s != z) & (s != below) & (s != above))
            def _():
                for u in range(2):
                    have(s, u)

        a = jnp.concatenate([data[2 * q], data[2 * q + 1]], axis=0)
        ah = a.astype(BF16)
        al = (a - ah.astype(F32)).astype(BF16)
        both = jnp.dot(wcat[...], ah, preferred_element_type=F32)
        outb[n] = both[0:NB] + both[NB:] + jnp.dot(wcat[0:NB], al, preferred_element_type=F32)
        for i in (2, 1, 3):
            other = lax.rem(x + i, NX)
            cp = remote(
                outb.at[n, pl.ds(pl.multiple_of(other * 32, 32), 32)],
                urecv.at[member, core, n],
                ex_send.at[i, n],
                ex_recv.at[member, core, n],
                dev(x + i, y, z, to_core),
            )
            cp.start()
            exchange.append(cp)
        own = outb.at[n, pl.ds(pl.multiple_of(x * 32, 32), 32)]

        @pl.when(to_core == core)
        def _():
            pltpu.make_async_copy(own, urecv.at[member, core, n], ex_recv.at[member, core, n]).start()

        @pl.when(to_core != core)
        def _():
            remote(
                own, urecv.at[member, core, n], ex_send.at[0, n], ex_recv.at[member, core, n], dev(x, y, z, 1 - core)
            ).start()

    steps = {"h": hop, "a": inv_along_z, "H": heads_along_x, "b": inv_along_x, "A": give, "B": pass_on, "W": weights, "C": chunk}
    for step in ORDER:
        steps[step[0]](*map(int, step[1:]))

    settle(stage.at[pl.ds(0, 3)], za_send.at[0])

    @pl.when(jnp.logical_not(active))
    def _():
        settle(stage.at[0], za_send.at[0])

    @pl.when(active)
    def _():
        settle(stage.at[pl.ds(0, NZ - 1)], sc_send.at[0])
        settle(panel_t.at[0, :, pl.ds(0, CW)], sc_send.at[0])

    @pl.when(active & (member == 1))
    def _():
        settle(panel_t.at[0, :, pl.ds(0, CW)], sc_send.at[0])

    settle(data.at[pl.ds(0, 7)], ag_send.at[0])

    settle(gath.at[pl.ds(0, NC - 1)], ga_send.at[0])
    settle(gath_head.at[pl.ds(0, NC - 1)], gh_send.at[0])
    settle(m_z.at[pl.ds(0, NZ - 1)], gb_send.at[0])
    settle(m_x.at[pl.ds(0, 3)], gc_send.at[0])
    settle(a_x.at[pl.ds(0, 3)], ax_send.at[0])

    even = lax.rem(lane, 2) == 0
    swap = lane + 1 - 2 * lax.rem(lane, 2)
    for n, q in enumerate(chunks):
        for h in range(2):
            for m in range(2):
                settle(urecv.at[m, h, n], ex_recv.at[m, h, n])
            for t in range(CW // 128):
                b = 24 * h + 2 * (q * (CW // 128) + t)
                for g in range(4):
                    u0 = urecv[0, h, n, g * 8 : (g + 1) * 8, t * 128 : (t + 1) * 128]
                    u1 = urecv[1, h, n, g * 8 : (g + 1) * 8, t * 128 : (t + 1) * 128]
                    low = jnp.where(even, u0, u1)
                    high = jnp.take_along_axis(jnp.where(even, u1, u0), swap, axis=1)
                    s0 = slab_t[g * 8 : (g + 1) * 8, pl.ds(pl.multiple_of(b * 128, 128), 128)]
                    s1 = slab_t[g * 8 : (g + 1) * 8, pl.ds(pl.multiple_of(b * 128 + 128, 128), 128)]
                    out_ref[pl.ds(g * 8 * 48 + b, 8, stride=48), :] = s0 - low
                    out_ref[pl.ds(g * 8 * 48 + b + 1, 8, stride=48), :] = s1 - high

        for cp in exchange[3 * n : 3 * n + 3]:
            cp.wait_send()

        @pl.when(to_core != core)
        def _():
            settle(outb.at[n, pl.ds(0, 32)], ex_send.at[0, n])


def body(inv_diag, panel, slab):
    dma = pltpu.SemaphoreType.DMA
    out = pl.pallas_call(
        kernel,
        out_shape=jax.ShapeDtypeStruct((1536, 128), F32),
        in_specs=[pl.BlockSpec(memory_space=pl.ANY)] * 3,
        out_specs=pl.BlockSpec(memory_space=pltpu.VMEM),
        scratch_shapes=[
            pltpu.VMEM((1, 4, 1, 8), F32),
            pltpu.VMEM((192, 128), F32),
            pltpu.VMEM((NQ, 8, 2 * CW), F32),
            pltpu.VMEM((1536, 128), F32),
            pltpu.VMEM((32, 6144), F32),
            pltpu.VMEM((8, 128), F32),
            pltpu.VMEM((8, 128), F32),
            pltpu.VMEM((NC, 8, 128), F32),
            pltpu.VMEM((NC, 8, 128), F32),
            pltpu.VMEM((NZ, 8, 128), F32),
            pltpu.VMEM((NX, 32, 128), F32),
            pltpu.VMEM((NX, NB, 128), F32),
            pltpu.VMEM((NZ, 8, 2 * CW), F32),
            pltpu.VMEM((NZ, NB // 2, CW), F32),
            pltpu.VMEM((NQ, NB, CW), F32),
            pltpu.VMEM((2, 2, NQ, 32, CW), F32),
            pltpu.VMEM((2 * NB, NB), BF16),
            dma((3,)),
            dma((1,)),
            dma((1,)),
            dma((1,)),
            dma((1,)),
            dma((1,)),
            dma((1,)),
            dma((1,)),
            dma((1,)),
            dma((1,)),
            dma((1,)),
            dma((1,)),
            dma((NZ,)),
            dma((1,)),
            dma((NZ, 2)),
            dma((1,)),
            dma((NX, NQ)),
            dma((2, 2, NQ)),
        ],
        compiler_params=pltpu.CompilerParams(
            collective_id=0, has_side_effects=True, vmem_limit_bytes=55_260_000
        ),
        cost_estimate=pl.CostEstimate(flops=200_000_000, bytes_accessed=1_700_000, transcendentals=0),
        name="panel_step",
    )(inv_diag, panel.reshape(192, 128), slab.reshape(1536, 128))
    return out.reshape(slab.shape)


def solution(mesh):
    return jax.shard_map(
        body,
        mesh=mesh,
        in_specs=(
            P("row", None, "col", None),
            P("col", None, "row", None),
            P("row", None, "col", None),
        ),
        out_specs=P("row", None, "col", None),
        check_vma=False,
    )
```

```python
import jax
import jax.numpy as jnp
from jax import lax
from jax.experimental import pallas as pl
from jax.experimental.pallas import tpu as pltpu
from jax.sharding import PartitionSpec as P

MESH = pl.DeviceIdType.MESH
NB = 128
NX, NY, NZ = 4, 8, 8
NC = 16
HALF = 1536
NQ = 4
CW = HALF // NQ
F32 = jnp.float32
BF16 = jnp.bfloat16
COLS = sorted(range(1, NC), key=lambda i: -min(i // 2, NY - i // 2))
ZS = (4, 3, 5, 2, 6, 1, 7)
PLACE = [c % 2 * 8 + c // 2 for c in range(NC)]
ORDER = (
    "h0", "h1", "h7", "h2", "h6", "h3", "h5", "a", "h4", "H",
    "A0", "b", "A1", "B0", "W", "C0", "B1", "C1", "C2", "C3",
)


def kernel(
    inv_ref,
    panel_ref,
    slab_ref,
    out_ref,
    panel_t,
    slab_lin,
    slab_t,
    mine,
    mine_head,
    gath,
    gath_head,
    m_z,
    m_x,
    a_x,
    stage,
    data,
    outb,
    urecv,
    wcat,
    in_sem,
    ga_send,
    ga_recv,
    gh_send,
    gh_recv,
    gb_send,
    gb_recv,
    gc_send,
    gc_recv,
    ax_send,
    ax_recv,
    za_send,
    za_recv,
    sc_send,
    blk_recv,
    ag_send,
    ex_send,
    ex_recv,
):
    row = lax.axis_index("row")
    col = lax.axis_index("col")
    x = lax.rem(row, NX)
    z = lax.div(row, NX)
    y = lax.div(col, 2)
    core = lax.rem(col, 2)

    def dev(dx, dy, dz, dk):
        return (lax.rem(dz, NZ) * NX + lax.rem(dx, NX), lax.rem(dy, NY) * 2 + dk)

    def remote(src, dst, ss, rs, device):
        return pltpu.make_async_remote_copy(
            src_ref=src, dst_ref=dst, send_sem=ss, recv_sem=rs, device_id=device, device_id_type=MESH
        )

    def settle(ref, sem):
        pltpu.make_async_copy(ref, ref, sem).wait()

    my_member = lax.div(z, 4)
    member = jnp.where(lax.div(x, 2) == lax.rem(y, 2), 0, 1)
    from_x = jnp.where(member == 0, x, 3 - x)
    from_z = lax.div(y, 2) + 4 * member
    to_core = lax.rem(from_x, 2)
    active = core == lax.rem(z, 2)

    loads = [
        pltpu.make_async_copy(slab_ref, slab_lin, in_sem.at[0]),
    ]
    for load in loads:
        load.start()

    barrier = pltpu.get_barrier_semaphore()

    def hello(device):
        pl.semaphore_signal(barrier, inc=1, device_id=device, device_id_type=MESH)

    for i in ZS:
        hello(dev(x, y, z + i, core))

    @pl.when(member == 1)
    def _():
        for i in (4, 3, 5, 2, 6, 1, 7, 0):
            hello(dev(from_x, y + i, z, lax.rem(z, 2)))

    for i in COLS:
        hello((row, lax.rem(col + i, NC)))
    for i in (2, 1, 3):
        hello(dev(x + i, y, z, core))

    lane = lax.broadcasted_iota(jnp.int32, (8, 128), 1)
    mine[...] = jnp.zeros_like(mine)
    for i in range(4):
        mine[i : i + 1, 0:8] = inv_ref[0, i, :, :]
    placed = pltpu.roll(pltpu.roll(mine[...], (core * 8 + y) * 8, 1), 4 * lax.rem(z, 2), 0)
    mine[...] = placed
    head = panel_ref[pl.ds(0, 8, stride=24), :]
    mine_head[...] = pltpu.roll(jnp.where(lane < 32, head, 0.0), x * 32, 1)
    gath_head[pl.ds(col, 1)] = mine_head[...].reshape(1, 8, 128)
    gath[pl.ds(col, 1)] = mine[...].reshape(1, 8, 128)
    perm = lax.div(lane, 2) + 64 * lax.rem(lane + my_member, 2)
    for q in range(NQ):
        for h in range(2):
            for t in range(3):
                tile = panel_ref[pl.ds(12 * h + 3 * q + t, 8, stride=24), :]
                panel_t[q, :, (3 * h + t) * 128 : (3 * h + t + 1) * 128] = jnp.take_along_axis(tile, perm, axis=1)

    pl.semaphore_wait(barrier, (NC - 1) + (NZ - 1) + (NX - 1) + jnp.where(active, 8, 0))

    for near, far in ((0, 1), (2, -1), (-2, 3), (4, -3)):
        zq = lax.rem(z + jnp.where(active, near, far) + NZ, NZ)
        piece_z = panel_t.at[lax.div(zq, 2)]

        @pl.when(zq == z)
        def _():
            pltpu.make_async_copy(piece_z, stage.at[z], za_recv.at[z]).start()

        @pl.when(zq != z)
        def _():
            remote(piece_z, stage.at[z], za_send.at[0], za_recv.at[z], dev(x, y, zq, core)).start()

    for i in COLS:
        remote(mine, gath.at[col], ga_send.at[0], ga_recv.at[0], (row, lax.rem(col + i, NC))).start()
    for i in COLS:
        remote(
            mine_head, gath_head.at[col], gh_send.at[0], gh_recv.at[0], (row, lax.rem(col + i, NC))
        ).start()

    loads[0].wait()
    for g in range(4):
        for b in range(48):
            slab_t[g * 8 : (g + 1) * 8, b * 128 : (b + 1) * 128] = slab_lin[pl.ds(g * 8 * 48 + b, 8, stride=48), :]

    my_rows = pl.ds(pl.multiple_of(y * 8, 8), 8)

    def hop(n):
        src = lax.rem(z + n, NZ)
        goes_x = jnp.where(src < 4, x, 3 - x)
        goes_y = 2 * lax.rem(src, 4) + lax.div(x, 2)
        at_home = (goes_x == x) & (goes_y == y)
        arrive = blk_recv.at[z, lax.div(y, 4)]

        @pl.when(active)
        def _():
            settle(stage.at[src], za_recv.at[src])
            for h in range(2):
                piece = stage.at[src, :, pl.ds(h * CW, CW)]

                @pl.when(at_home & (core == h))
                def _():
                    pltpu.make_async_copy(piece, data.at[z, my_rows], arrive).start()

                @pl.when(jnp.logical_not(at_home & (core == h)))
                def _():
                    remote(piece, data.at[z, my_rows], sc_send.at[0], arrive, dev(goes_x, goes_y, z, h)).start()

    def inv_along_z():
        settle(gath.at[pl.ds(0, NC - 1)], ga_recv.at[0])
        rows = gath[0]
        for i in range(1, NC):
            rows = rows + gath[i]
        m_z[pl.ds(z, 1)] = rows.reshape(1, 8, 128)
        for i in ZS:
            remote(m_z.at[z], m_z.at[z], gb_send.at[0], gb_recv.at[0], dev(x, y, z + i, core)).start()

    def heads_along_x():
        settle(gath_head.at[pl.ds(0, NC - 1)], gh_recv.at[0])
        for i in range(NC):
            a_x[x, PLACE[i] * 8 : (PLACE[i] + 1) * 8, :] = gath_head[i]
        for i in (2, 1, 3):
            remote(a_x.at[x], a_x.at[x], ax_send.at[0], ax_recv.at[0], dev(x + i, y, z, core)).start()

    def inv_along_x():
        settle(m_z.at[pl.ds(0, NZ - 1)], gb_recv.at[0])
        for j in range(4):
            m_x[x, j * 8 : (j + 1) * 8, :] = m_z[2 * j] + m_z[2 * j + 1]
        for i in (2, 1, 3):
            remote(m_x.at[x], m_x.at[x], gc_send.at[0], gc_recv.at[0], dev(x + i, y, z, core)).start()

    def block(s, u):
        return data.at[s, pl.ds(pl.multiple_of(u * 32, 32), 32)]

    def have(s, u):
        settle(block(s, u), blk_recv.at[s, u])

    def share(s, u, dz):
        remote(block(s, u), block(s, u), ag_send.at[0], blk_recv.at[s, u], dev(x, y, z + dz + NZ, core)).start()

    subs = [lax.div(y, 4), 1 - lax.div(y, 4)]
    below = lax.rem(z + NZ - 2, NZ)
    above = lax.rem(z + 2, NZ)

    def give(i):
        have(z, subs[i])
        for dz in (1, -1, 2, -2):
            share(z, subs[i], dz)

    def pass_on(i):
        have(below, subs[i])
        for dz in (2, 1) if i == 0 else (1,):
            share(below, subs[i], dz)
        have(above, subs[i])
        for dz in (-2, -1) if i == 1 else (-1,):
            share(above, subs[i], dz)

    def weights():
        settle(a_x.at[pl.ds(0, 3)], ax_recv.at[0])
        heads = (a_x[0] + a_x[1] + a_x[2] + a_x[3]).T
        settle(m_x.at[pl.ds(0, 3)], gc_recv.at[0])
        inverse = m_x[...].reshape(NB, NB)
        gram = jnp.dot(inverse.T, inverse, precision=lax.Precision.HIGHEST, preferred_element_type=F32)
        w = jnp.dot(heads, gram, precision=lax.Precision.HIGHEST, preferred_element_type=F32)
        wh = w.astype(BF16)
        wcat[0:NB] = wh
        wcat[NB:] = (w - wh.astype(F32)).astype(BF16)

    mine_q = lax.div(z, 2)
    lean = jnp.where(lax.rem(z, 2) == 0, 3, 1)
    chunks = [mine_q, lax.rem(mine_q + lean, NQ), lax.rem(mine_q + 4 - lean, NQ), lax.rem(mine_q + 2, NQ)]
    exchange = []

    def chunk(n):
        q = chunks[n]
        for half in range(2):
            s = 2 * q + half

            @pl.when((s != z) & (s != below) & (s != above))
            def _():
                for u in range(2):
                    have(s, u)

        a = jnp.concatenate([data[2 * q], data[2 * q + 1]], axis=0)
        ah = a.astype(BF16)
        al = (a - ah.astype(F32)).astype(BF16)
        both = jnp.dot(wcat[...], ah, preferred_element_type=F32)
        outb[n] = both[0:NB] + both[NB:] + jnp.dot(wcat[0:NB], al, preferred_element_type=F32)
        for i in (2, 1, 3):
            other = lax.rem(x + i, NX)
            cp = remote(
                outb.at[n, pl.ds(pl.multiple_of(other * 32, 32), 32)],
                urecv.at[member, core, n],
                ex_send.at[i, n],
                ex_recv.at[member, core, n],
                dev(x + i, y, z, to_core),
            )
            cp.start()
            exchange.append(cp)
        own = outb.at[n, pl.ds(pl.multiple_of(x * 32, 32), 32)]

        @pl.when(to_core == core)
        def _():
            pltpu.make_async_copy(own, urecv.at[member, core, n], ex_recv.at[member, core, n]).start()

        @pl.when(to_core != core)
        def _():
            remote(
                own, urecv.at[member, core, n], ex_send.at[0, n], ex_recv.at[member, core, n], dev(x, y, z, 1 - core)
            ).start()

    steps = {"h": hop, "a": inv_along_z, "H": heads_along_x, "b": inv_along_x, "A": give, "B": pass_on, "W": weights, "C": chunk}
    for step in ORDER:
        steps[step[0]](*map(int, step[1:]))

    settle(stage.at[pl.ds(0, 3)], za_send.at[0])

    @pl.when(jnp.logical_not(active))
    def _():
        settle(stage.at[0], za_send.at[0])

    @pl.when(active)
    def _():
        settle(stage.at[pl.ds(0, NZ - 1)], sc_send.at[0])
        settle(panel_t.at[0, :, pl.ds(0, CW)], sc_send.at[0])

    @pl.when(active & (member == 1))
    def _():
        settle(panel_t.at[0, :, pl.ds(0, CW)], sc_send.at[0])

    settle(data.at[pl.ds(0, 7)], ag_send.at[0])

    settle(gath.at[pl.ds(0, NC - 1)], ga_send.at[0])
    settle(gath_head.at[pl.ds(0, NC - 1)], gh_send.at[0])
    settle(m_z.at[pl.ds(0, NZ - 1)], gb_send.at[0])
    settle(m_x.at[pl.ds(0, 3)], gc_send.at[0])
    settle(a_x.at[pl.ds(0, 3)], ax_send.at[0])

    even = lax.rem(lane, 2) == 0
    swap = lane + 1 - 2 * lax.rem(lane, 2)
    for n, q in enumerate(chunks):
        for h in range(2):
            for m in range(2):
                settle(urecv.at[m, h, n], ex_recv.at[m, h, n])
            for t in range(CW // 128):
                b = 24 * h + 2 * (q * (CW // 128) + t)
                for g in range(4):
                    u0 = urecv[0, h, n, g * 8 : (g + 1) * 8, t * 128 : (t + 1) * 128]
                    u1 = urecv[1, h, n, g * 8 : (g + 1) * 8, t * 128 : (t + 1) * 128]
                    low = jnp.where(even, u0, u1)
                    high = jnp.take_along_axis(jnp.where(even, u1, u0), swap, axis=1)
                    s0 = slab_t[g * 8 : (g + 1) * 8, pl.ds(pl.multiple_of(b * 128, 128), 128)]
                    s1 = slab_t[g * 8 : (g + 1) * 8, pl.ds(pl.multiple_of(b * 128 + 128, 128), 128)]
                    out_ref[pl.ds(g * 8 * 48 + b, 8, stride=48), :] = s0 - low
                    out_ref[pl.ds(g * 8 * 48 + b + 1, 8, stride=48), :] = s1 - high

        for cp in exchange[3 * n : 3 * n + 3]:
            cp.wait_send()

        @pl.when(to_core != core)
        def _():
            settle(outb.at[n, pl.ds(0, 32)], ex_send.at[0, n])


def body(inv_diag, panel, slab):
    dma = pltpu.SemaphoreType.DMA
    out = pl.pallas_call(
        kernel,
        out_shape=jax.ShapeDtypeStruct((1536, 128), F32),
        in_specs=[pl.BlockSpec(memory_space=pltpu.VMEM)] * 2 + [pl.BlockSpec(memory_space=pl.ANY)],
        out_specs=pl.BlockSpec(memory_space=pltpu.VMEM),
        scratch_shapes=[
            pltpu.VMEM((NQ, 8, 2 * CW), F32),
            pltpu.VMEM((1536, 128), F32),
            pltpu.VMEM((32, 6144), F32),
            pltpu.VMEM((8, 128), F32),
            pltpu.VMEM((8, 128), F32),
            pltpu.VMEM((NC, 8, 128), F32),
            pltpu.VMEM((NC, 8, 128), F32),
            pltpu.VMEM((NZ, 8, 128), F32),
            pltpu.VMEM((NX, 32, 128), F32),
            pltpu.VMEM((NX, NB, 128), F32),
            pltpu.VMEM((NZ, 8, 2 * CW), F32),
            pltpu.VMEM((NZ, NB // 2, CW), F32),
            pltpu.VMEM((NQ, NB, CW), F32),
            pltpu.VMEM((2, 2, NQ, 32, CW), F32),
            pltpu.VMEM((2 * NB, NB), BF16),
            dma((1,)),
            dma((1,)),
            dma((1,)),
            dma((1,)),
            dma((1,)),
            dma((1,)),
            dma((1,)),
            dma((1,)),
            dma((1,)),
            dma((1,)),
            dma((1,)),
            dma((1,)),
            dma((NZ,)),
            dma((1,)),
            dma((NZ, 2)),
            dma((1,)),
            dma((NX, NQ)),
            dma((2, 2, NQ)),
        ],
        compiler_params=pltpu.CompilerParams(
            collective_id=0, has_side_effects=True, vmem_limit_bytes=55_260_000
        ),
        cost_estimate=pl.CostEstimate(flops=200_000_000, bytes_accessed=1_700_000, transcendentals=0),
        name="panel_step",
    )(inv_diag, panel.reshape(192, 128), slab.reshape(1536, 128))
    return out.reshape(slab.shape)


def solution(mesh):
    return jax.shard_map(
        body,
        mesh=mesh,
        in_specs=(
            P("row", None, "col", None),
            P("col", None, "row", None),
            P("row", None, "col", None),
        ),
        out_specs=P("row", None, "col", None),
        check_vma=False,
    )
```

```python
import jax
import jax.numpy as jnp
from jax import lax
from jax.experimental import pallas as pl
from jax.experimental.pallas import tpu as pltpu
from jax.sharding import PartitionSpec as P

MESH = pl.DeviceIdType.MESH
NB = 128
NX, NY, NZ = 4, 8, 8
NC = 16
HALF = 1536
NQ = 4
CW = HALF // NQ
F32 = jnp.float32
BF16 = jnp.bfloat16
COLS = sorted(range(1, NC), key=lambda i: -min(i // 2, NY - i // 2))
ZS = (4, 3, 5, 2, 6, 1, 7)
PLACE = [c % 2 * 8 + c // 2 for c in range(NC)]
ORDER = (
    "h0", "h1", "h7", "E", "h2", "h6", "h3", "h5", "a", "h4", "H",
    "A0", "b", "A1", "B0", "W", "C0", "B1", "C1", "C2", "C3",
)


def kernel(
    inv_ref,
    panel_ref,
    slab_ref,
    out_ref,
    panel_t,
    slab_lin,
    slab_t,
    mine,
    mine_head,
    gath,
    gath_head,
    m_z,
    m_x,
    a_x,
    stage,
    data,
    outb,
    urecv,
    wcat,
    in_sem,
    ga_send,
    ga_recv,
    gh_send,
    gh_recv,
    gb_send,
    gb_recv,
    gc_send,
    gc_recv,
    ax_send,
    ax_recv,
    za_send,
    za_recv,
    sc_send,
    blk_recv,
    ag_send,
    ex_send,
    ex_recv,
):
    row = lax.axis_index("row")
    col = lax.axis_index("col")
    x = lax.rem(row, NX)
    z = lax.div(row, NX)
    y = lax.div(col, 2)
    core = lax.rem(col, 2)

    def dev(dx, dy, dz, dk):
        return (lax.rem(dz, NZ) * NX + lax.rem(dx, NX), lax.rem(dy, NY) * 2 + dk)

    def remote(src, dst, ss, rs, device):
        return pltpu.make_async_remote_copy(
            src_ref=src, dst_ref=dst, send_sem=ss, recv_sem=rs, device_id=device, device_id_type=MESH
        )

    def settle(ref, sem):
        pltpu.make_async_copy(ref, ref, sem).wait()

    my_member = lax.div(z, 4)
    member = jnp.where(lax.div(x, 2) == lax.rem(y, 2), 0, 1)
    from_x = jnp.where(member == 0, x, 3 - x)
    from_z = lax.div(y, 2) + 4 * member
    to_core = lax.rem(from_x, 2)
    active = core == lax.rem(z, 2)

    loads = [
        pltpu.make_async_copy(slab_ref, slab_lin, in_sem.at[0]),
    ]
    for load in loads:
        load.start()

    barrier = pltpu.get_barrier_semaphore()

    def hello(device):
        pl.semaphore_signal(barrier, inc=1, device_id=device, device_id_type=MESH)

    for i in ZS:
        hello(dev(x, y, z + i, core))

    @pl.when(member == 1)
    def _():
        for i in (4, 3, 5, 2, 6, 1, 7, 0):
            hello(dev(from_x, y + i, z, lax.rem(z, 2)))

    for i in COLS:
        hello((row, lax.rem(col + i, NC)))
    for i in (2, 1, 3):
        hello(dev(x + i, y, z, core))

    lane = lax.broadcasted_iota(jnp.int32, (8, 128), 1)
    mine[...] = jnp.zeros_like(mine)
    for i in range(4):
        mine[i : i + 1, 0:8] = inv_ref[0, i, :, :]
    placed = pltpu.roll(pltpu.roll(mine[...], (core * 8 + y) * 8, 1), 4 * lax.rem(z, 2), 0)
    mine[...] = placed
    head = panel_ref[pl.ds(0, 8, stride=24), :]
    mine_head[...] = pltpu.roll(jnp.where(lane < 32, head, 0.0), x * 32, 1)
    gath_head[pl.ds(col, 1)] = mine_head[...].reshape(1, 8, 128)
    gath[pl.ds(col, 1)] = mine[...].reshape(1, 8, 128)
    perm = lax.div(lane, 2) + 64 * lax.rem(lane + my_member, 2)
    for q in range(NQ):
        for h in range(2):
            for t in range(3):
                tile = panel_ref[pl.ds(12 * h + 3 * q + t, 8, stride=24), :]
                panel_t[q, :, (3 * h + t) * 128 : (3 * h + t + 1) * 128] = jnp.take_along_axis(tile, perm, axis=1)

    pl.semaphore_wait(barrier, (NC - 1) + (NZ - 1) + (NX - 1) + jnp.where(active, 8, 0))

    for near, far in ((0, 1), (2, -1), (-2, 3), (4, -3)):
        zq = lax.rem(z + jnp.where(active, near, far) + NZ, NZ)
        piece_z = panel_t.at[lax.div(zq, 2)]

        @pl.when(zq == z)
        def _():
            pltpu.make_async_copy(piece_z, stage.at[z], za_recv.at[z]).start()

        @pl.when(zq != z)
        def _():
            remote(piece_z, stage.at[z], za_send.at[0], za_recv.at[z], dev(x, y, zq, core)).start()

    for i in COLS:
        remote(mine, gath.at[col], ga_send.at[0], ga_recv.at[0], (row, lax.rem(col + i, NC))).start()

    loads[0].wait()
    for g in range(4):
        for b in range(48):
            slab_t[g * 8 : (g + 1) * 8, b * 128 : (b + 1) * 128] = slab_lin[pl.ds(g * 8 * 48 + b, 8, stride=48), :]

    my_rows = pl.ds(pl.multiple_of(y * 8, 8), 8)

    def hop(n):
        src = lax.rem(z + n, NZ)
        goes_x = jnp.where(src < 4, x, 3 - x)
        goes_y = 2 * lax.rem(src, 4) + lax.div(x, 2)
        at_home = (goes_x == x) & (goes_y == y)
        arrive = blk_recv.at[z, lax.div(y, 4)]

        @pl.when(active)
        def _():
            settle(stage.at[src], za_recv.at[src])
            for h in range(2):
                piece = stage.at[src, :, pl.ds(h * CW, CW)]

                @pl.when(at_home & (core == h))
                def _():
                    pltpu.make_async_copy(piece, data.at[z, my_rows], arrive).start()

                @pl.when(jnp.logical_not(at_home & (core == h)))
                def _():
                    remote(piece, data.at[z, my_rows], sc_send.at[0], arrive, dev(goes_x, goes_y, z, h)).start()

    def inv_along_z():
        settle(gath.at[pl.ds(0, NC - 1)], ga_recv.at[0])
        rows = gath[0]
        for i in range(1, NC):
            rows = rows + gath[i]
        m_z[pl.ds(z, 1)] = rows.reshape(1, 8, 128)
        for i in ZS:
            remote(m_z.at[z], m_z.at[z], gb_send.at[0], gb_recv.at[0], dev(x, y, z + i, core)).start()

    def heads_along_x():
        settle(gath_head.at[pl.ds(0, NC - 1)], gh_recv.at[0])
        for i in range(NC):
            a_x[x, PLACE[i] * 8 : (PLACE[i] + 1) * 8, :] = gath_head[i]
        for i in (2, 1, 3):
            remote(a_x.at[x], a_x.at[x], ax_send.at[0], ax_recv.at[0], dev(x + i, y, z, core)).start()

    def inv_along_x():
        settle(m_z.at[pl.ds(0, NZ - 1)], gb_recv.at[0])
        for j in range(4):
            m_x[x, j * 8 : (j + 1) * 8, :] = m_z[2 * j] + m_z[2 * j + 1]
        for i in (2, 1, 3):
            remote(m_x.at[x], m_x.at[x], gc_send.at[0], gc_recv.at[0], dev(x + i, y, z, core)).start()

    def block(s, u):
        return data.at[s, pl.ds(pl.multiple_of(u * 32, 32), 32)]

    def have(s, u):
        settle(block(s, u), blk_recv.at[s, u])

    def share(s, u, dz):
        remote(block(s, u), block(s, u), ag_send.at[0], blk_recv.at[s, u], dev(x, y, z + dz + NZ, core)).start()

    subs = [lax.div(y, 4), 1 - lax.div(y, 4)]
    below = lax.rem(z + NZ - 2, NZ)
    above = lax.rem(z + 2, NZ)

    def give(i):
        have(z, subs[i])
        for dz in (1, -1, 2, -2):
            share(z, subs[i], dz)

    def pass_on(i):
        have(below, subs[i])
        for dz in (2, 1) if i == 0 else (1,):
            share(below, subs[i], dz)
        have(above, subs[i])
        for dz in (-2, -1) if i == 1 else (-1,):
            share(above, subs[i], dz)

    def weights():
        settle(a_x.at[pl.ds(0, 3)], ax_recv.at[0])
        heads = (a_x[0] + a_x[1] + a_x[2] + a_x[3]).T
        settle(m_x.at[pl.ds(0, 3)], gc_recv.at[0])
        inverse = m_x[...].reshape(NB, NB)
        gram = jnp.dot(inverse.T, inverse, precision=lax.Precision.HIGHEST, preferred_element_type=F32)
        w = jnp.dot(heads, gram, precision=lax.Precision.HIGHEST, preferred_element_type=F32)
        wh = w.astype(BF16)
        wcat[0:NB] = wh
        wcat[NB:] = (w - wh.astype(F32)).astype(BF16)

    mine_q = lax.div(z, 2)
    lean = jnp.where(lax.rem(z, 2) == 0, 3, 1)
    chunks = [mine_q, lax.rem(mine_q + lean, NQ), lax.rem(mine_q + 4 - lean, NQ), lax.rem(mine_q + 2, NQ)]
    exchange = []

    def chunk(n):
        q = chunks[n]
        for half in range(2):
            s = 2 * q + half

            @pl.when((s != z) & (s != below) & (s != above))
            def _():
                for u in range(2):
                    have(s, u)

        a = jnp.concatenate([data[2 * q], data[2 * q + 1]], axis=0)
        ah = a.astype(BF16)
        al = (a - ah.astype(F32)).astype(BF16)
        both = jnp.dot(wcat[...], ah, preferred_element_type=F32)
        outb[n] = both[0:NB] + both[NB:] + jnp.dot(wcat[0:NB], al, preferred_element_type=F32)
        for i in (2, 1, 3):
            other = lax.rem(x + i, NX)
            cp = remote(
                outb.at[n, pl.ds(pl.multiple_of(other * 32, 32), 32)],
                urecv.at[member, core, n],
                ex_send.at[i, n],
                ex_recv.at[member, core, n],
                dev(x + i, y, z, to_core),
            )
            cp.start()
            exchange.append(cp)
        own = outb.at[n, pl.ds(pl.multiple_of(x * 32, 32), 32)]

        @pl.when(to_core == core)
        def _():
            pltpu.make_async_copy(own, urecv.at[member, core, n], ex_recv.at[member, core, n]).start()

        @pl.when(to_core != core)
        def _():
            remote(
                own, urecv.at[member, core, n], ex_send.at[0, n], ex_recv.at[member, core, n], dev(x, y, z, 1 - core)
            ).start()

    def send_heads():
        for i in COLS:
            remote(
                mine_head, gath_head.at[col], gh_send.at[0], gh_recv.at[0], (row, lax.rem(col + i, NC))
            ).start()

    steps = {"E": send_heads, "h": hop, "a": inv_along_z, "H": heads_along_x, "b": inv_along_x, "A": give, "B": pass_on, "W": weights, "C": chunk}
    for step in ORDER:
        steps[step[0]](*map(int, step[1:]))

    settle(stage.at[pl.ds(0, 3)], za_send.at[0])

    @pl.when(jnp.logical_not(active))
    def _():
        settle(stage.at[0], za_send.at[0])

    @pl.when(active)
    def _():
        settle(stage.at[pl.ds(0, NZ - 1)], sc_send.at[0])
        settle(panel_t.at[0, :, pl.ds(0, CW)], sc_send.at[0])

    @pl.when(active & (member == 1))
    def _():
        settle(panel_t.at[0, :, pl.ds(0, CW)], sc_send.at[0])

    settle(data.at[pl.ds(0, 7)], ag_send.at[0])

    settle(gath.at[pl.ds(0, NC - 1)], ga_send.at[0])
    settle(gath_head.at[pl.ds(0, NC - 1)], gh_send.at[0])
    settle(m_z.at[pl.ds(0, NZ - 1)], gb_send.at[0])
    settle(m_x.at[pl.ds(0, 3)], gc_send.at[0])
    settle(a_x.at[pl.ds(0, 3)], ax_send.at[0])

    even = lax.rem(lane, 2) == 0
    swap = lane + 1 - 2 * lax.rem(lane, 2)
    for n, q in enumerate(chunks):
        for h in range(2):
            for m in range(2):
                settle(urecv.at[m, h, n], ex_recv.at[m, h, n])
            for t in range(CW // 128):
                b = 24 * h + 2 * (q * (CW // 128) + t)
                for g in range(4):
                    u0 = urecv[0, h, n, g * 8 : (g + 1) * 8, t * 128 : (t + 1) * 128]
                    u1 = urecv[1, h, n, g * 8 : (g + 1) * 8, t * 128 : (t + 1) * 128]
                    low = jnp.where(even, u0, u1)
                    high = jnp.take_along_axis(jnp.where(even, u1, u0), swap, axis=1)
                    s0 = slab_t[g * 8 : (g + 1) * 8, pl.ds(pl.multiple_of(b * 128, 128), 128)]
                    s1 = slab_t[g * 8 : (g + 1) * 8, pl.ds(pl.multiple_of(b * 128 + 128, 128), 128)]
                    out_ref[pl.ds(g * 8 * 48 + b, 8, stride=48), :] = s0 - low
                    out_ref[pl.ds(g * 8 * 48 + b + 1, 8, stride=48), :] = s1 - high

        for cp in exchange[3 * n : 3 * n + 3]:
            cp.wait_send()

        @pl.when(to_core != core)
        def _():
            settle(outb.at[n, pl.ds(0, 32)], ex_send.at[0, n])


def body(inv_diag, panel, slab):
    dma = pltpu.SemaphoreType.DMA
    out = pl.pallas_call(
        kernel,
        out_shape=jax.ShapeDtypeStruct((1536, 128), F32),
        in_specs=[pl.BlockSpec(memory_space=pltpu.VMEM)] * 2 + [pl.BlockSpec(memory_space=pl.ANY)],
        out_specs=pl.BlockSpec(memory_space=pltpu.VMEM),
        scratch_shapes=[
            pltpu.VMEM((NQ, 8, 2 * CW), F32),
            pltpu.VMEM((1536, 128), F32),
            pltpu.VMEM((32, 6144), F32),
            pltpu.VMEM((8, 128), F32),
            pltpu.VMEM((8, 128), F32),
            pltpu.VMEM((NC, 8, 128), F32),
            pltpu.VMEM((NC, 8, 128), F32),
            pltpu.VMEM((NZ, 8, 128), F32),
            pltpu.VMEM((NX, 32, 128), F32),
            pltpu.VMEM((NX, NB, 128), F32),
            pltpu.VMEM((NZ, 8, 2 * CW), F32),
            pltpu.VMEM((NZ, NB // 2, CW), F32),
            pltpu.VMEM((NQ, NB, CW), F32),
            pltpu.VMEM((2, 2, NQ, 32, CW), F32),
            pltpu.VMEM((2 * NB, NB), BF16),
            dma((1,)),
            dma((1,)),
            dma((1,)),
            dma((1,)),
            dma((1,)),
            dma((1,)),
            dma((1,)),
            dma((1,)),
            dma((1,)),
            dma((1,)),
            dma((1,)),
            dma((1,)),
            dma((NZ,)),
            dma((1,)),
            dma((NZ, 2)),
            dma((1,)),
            dma((NX, NQ)),
            dma((2, 2, NQ)),
        ],
        compiler_params=pltpu.CompilerParams(
            collective_id=0, has_side_effects=True, vmem_limit_bytes=55_260_000
        ),
        cost_estimate=pl.CostEstimate(flops=200_000_000, bytes_accessed=1_700_000, transcendentals=0),
        name="panel_step",
    )(inv_diag, panel.reshape(192, 128), slab.reshape(1536, 128))
    return out.reshape(slab.shape)


def solution(mesh):
    return jax.shard_map(
        body,
        mesh=mesh,
        in_specs=(
            P("row", None, "col", None),
            P("col", None, "row", None),
            P("row", None, "col", None),
        ),
        out_specs=P("row", None, "col", None),
        check_vma=False,
    )
```
